128 devices in a mesh: seq: 16 (over z, y), tp: 8 (over x, core).
Axes of the slice: x: 4, y: 4, z: 4, core: 2. Of those that a mesh axis runs over, the one named last changes fastest.
Arguments:
- queries: bfloat16 [8192, 4096], P('seq', 'tp'), may hold values from -8 to 8
- nb_keys: bfloat16 [32768, 4096], P('seq', 'tp'), may hold values from -8 to 8
- nb_values: bfloat16 [32768, 4096], P('seq', 'tp'), may hold values from -6 to 6
- out_weight: bfloat16 [4096, 8192], P('tp'), may hold values from -0.09375 to 0.09375
- out_grad: bfloat16 [8192, 8192], P(('seq', 'tp')), may hold values from -6 to 6
- span_refs: int32 [128, 2], P('seq'), may hold values from 0 to 31, as said below
- block_dest: int32 [256], P('seq'), may hold values from 0 to 15, as said below
- block_valid: int32 [256], P('seq'), may hold values from 32 to 128, as said below
Outputs:
- mixed: bfloat16 [8192, 8192], P(('seq', 'tp'))
- d_queries: bfloat16 [8192, 4096], P('seq', 'tp')
- d_keys: bfloat16 [32768, 4096], P('seq', 'tp')
- d_values: bfloat16 [32768, 4096], P('seq', 'tp')
The draws below stay inside these ranges and needn't reach their ends.
Inputs may be any that keep to these rules, and one draw needn't show every extreme that they name: `block_dest`: each index of seq sends its blocks to 8 distinct owners, exactly 2 blocks to each; one of them is its own index, and 4 owners drawn afresh receive 2 blocks from every index. `span_refs`: the two slots of a span differ, and each holds a block sent to that span's owner: slot s * 2 + c holds the block of rank c that index s sends there. `block_valid`: the first block of every index of seq has all 128 rows valid.
All inputs are finite; a program needn't handle non-finite values.
Results may differ from the reference program's by a relative error of at most 0.017.
Values may be sent and summed in bfloat16 or wider, within the bound.
No kernel may reach another device: no remote copies, remote signals or barrier semaphores. Data moves between devices by JAX's collectives and lax.ppermute only.
A program may use at most 128 MiB of HBM per device.

```python
import jax
import jax.numpy as jnp
from jax import lax

D = 8192
HEADS = 32
HD = 128
SPAN = 64
BR = 128
NEIGH = 2
CAP = 2
CH_DEV = 8
NB_DEV = 16
TOKENS = 8192
NBLOCKS = 256
N_SEQ = 16
N_TP = 8


def routing(key):
    hot_key, score_key, order_key, one_key, two_key = jax.random.split(key, 5)
    hot_rank = jnp.argsort(jax.random.permutation(hot_key, N_SEQ))
    heaviest_holder_chip = hot_rank < N_SEQ // 4
    resident_holder_chip = jnp.eye(N_SEQ, dtype=bool)
    merit_marks = jax.random.randint(score_key, (N_SEQ, N_SEQ), 0, 65536)
    extra_credit_marks = jnp.where(heaviest_holder_chip[None, :] | resident_holder_chip, 131072, 0)
    graded_sequence = (merit_marks + extra_credit_marks) * N_SEQ + jnp.arange(N_SEQ)[None, :]
    ranked_top, chosen = lax.top_k(graded_sequence, NB_DEV // CAP)
    shuffle = jax.random.randint(order_key, (N_SEQ, NB_DEV), 0, 65536) * NB_DEV + jnp.arange(NB_DEV)[None, :]
    places = jnp.argsort(shuffle, axis=1)
    owner_lookup = jnp.take_along_axis(chosen, places // CAP, axis=1).astype(jnp.int32)
    sent_count = jnp.sum((owner_lookup[:, :, None] == jnp.arange(N_SEQ)[None, None, :]).astype(jnp.int32), axis=1)
    filled = jnp.transpose(sent_count)[:, :, None] > jnp.arange(CAP)[None, None, :]
    filled = filled.reshape(N_SEQ, N_SEQ * CAP).astype(jnp.int32)
    filled_upto = jnp.cumsum(filled, axis=1)
    filled_count = jnp.repeat(filled_upto[:, -1], CH_DEV)
    pick_one = jax.random.randint(one_key, (N_SEQ * CH_DEV,), 0, filled_count)
    pick_two = (pick_one + 1 + jax.random.randint(two_key, (N_SEQ * CH_DEV,), 0, filled_count - 1)) % filled_count
    span_upto = jnp.repeat(filled_upto, CH_DEV, axis=0)

    def locate(rank_wanted):
        return jnp.sum((span_upto <= rank_wanted[:, None]).astype(jnp.int32), axis=1)
    span_slots = jnp.stack([locate(pick_one), locate(pick_two)], axis=1).astype(jnp.int32)
    return (owner_lookup.reshape(-1), span_slots)


def draw_block_dest(key, part):
    owner_lookup, span_slots = routing(key)
    return owner_lookup


def draw_span_refs(key, part):
    owner_lookup, span_slots = routing(key)
    return span_slots


def draw_block_valid(key, part):
    key = jax.random.fold_in(key, 7)
    rows_drawn = jax.random.randint(key, (NBLOCKS,), BR // 4, BR + 1)
    first_block = jnp.arange(NBLOCKS) % NB_DEV == 0
    return jnp.where(first_block, BR, rows_drawn).astype(jnp.int32)


def draw_queries(key, part):
    key = jax.random.fold_in(key, 11)
    base_key = jax.random.fold_in(key, 0)
    values_base = jnp.clip(jax.random.normal(base_key, (TOKENS, HEADS * HD), jnp.float32), -6.0, 6.0)
    return values_base.astype(jnp.bfloat16)


def draw_nb_keys(key, part):
    key = jax.random.fold_in(key, 13)
    values_base = jnp.clip(jax.random.normal(key, (NBLOCKS * BR, HEADS * HD), jnp.float32), -6.0, 6.0)
    return values_base.astype(jnp.bfloat16)


def levels(own_key, extent, pieces, least, high):
    def one(axis_at, parts):
        steps = jax.random.uniform(jax.random.fold_in(jax.random.fold_in(own_key, 6), axis_at), (parts,), jnp.float32, least / len(pieces), high / len(pieces))
        return jnp.repeat(jnp.exp(steps), extent[axis_at] // parts).reshape((-1,) + (1,) * (len(extent) - axis_at - 1))

    factor_of = one(*pieces[0])
    for cut in pieces[1:]:
        factor_of = factor_of * one(*cut)
    return factor_of


def bell_draw(stream_key, extent, width, bound, cuts=(), held_as=jnp.bfloat16):
    level = levels(stream_key, extent, cuts, -0.22, 0.18) if cuts else 1.0
    array = jax.random.normal(stream_key, extent, jnp.float32) * width * level
    return jnp.minimum(jnp.maximum(array, -bound), bound).astype(held_as)


def setup_inputs(seed: int = 0) -> dict:
    seeds = jax.random.split(jax.random.key(seed), 9)
    return {
        "queries": draw_queries(jax.random.fold_in(seeds[8], 71), 0),
        "nb_keys": draw_nb_keys(jax.random.fold_in(seeds[8], 71), 0),
        "nb_values": bell_draw(seeds[2], (NBLOCKS * BR, HEADS * HD), 1.0, 6.0, ((0, 16), (1, 8))),
        "out_weight": bell_draw(seeds[3], (HEADS * HD, D), (HEADS * HD) ** -0.5, 0.09375, ((0, 8),)),
        "out_grad": bell_draw(seeds[4], (TOKENS, D), 1.0, 6.0, ((0, 128),)),
        "span_refs": draw_span_refs(jax.random.fold_in(seeds[8], 71), 0),
        "block_dest": draw_block_dest(jax.random.fold_in(seeds[8], 71), 0),
        "block_valid": draw_block_valid(jax.random.fold_in(seeds[8], 71), 0),
    }


def reference(queries, nb_keys, nb_values, out_weight, out_grad, span_refs, block_dest, block_valid):
    col_width = HEADS * HD // N_TP
    group_heads = HEADS // N_TP
    span_count = N_SEQ * CH_DEV
    block_count = N_SEQ * NB_DEV
    score_scale = HD ** -0.5
    owner_lookup = block_dest.reshape(N_SEQ, NB_DEV).astype(jnp.int32)
    same_owner = owner_lookup[:, :, None] == owner_lookup[:, None, :]
    before = jnp.arange(NB_DEV)[:, None] < jnp.arange(NB_DEV)[None, :]
    slot_rank = jnp.sum((same_owner & before[None]).astype(jnp.int32), axis=1).astype(jnp.int32)
    sender = jnp.arange(N_SEQ, dtype=jnp.int32)[:, None]
    block_ids = sender * NB_DEV + jnp.arange(NB_DEV, dtype=jnp.int32)[None, :]
    slot_table = jnp.zeros((N_SEQ, N_SEQ * CAP), jnp.int32).at[owner_lookup, sender * CAP + slot_rank].set(block_ids)
    owner_ids = (jnp.arange(span_count, dtype=jnp.int32) // CH_DEV).astype(jnp.int32)
    span_blocks = slot_table[owner_ids[:, None], span_refs.astype(jnp.int32)].astype(jnp.int32)
    valid_rows = block_valid[span_blocks]
    live_keys = (jnp.arange(BR, dtype=jnp.int32)[None, None, :] < valid_rows[:, :, None]).reshape(span_count, NEIGH * BR)
    live_mask = live_keys[:, None, None, :]

    def head_group(index):
        col_start = index * col_width
        query_rows = lax.dynamic_slice_in_dim(queries, col_start, col_width, 1)
        query_rows = query_rows.reshape(span_count, SPAN, group_heads, HD).astype(jnp.float32)
        key_all = lax.dynamic_slice_in_dim(nb_keys, col_start, col_width, 1).reshape(block_count, BR, group_heads, HD)
        every_payload_vector = lax.dynamic_slice_in_dim(nb_values, col_start, col_width, 1).reshape(block_count, BR, group_heads, HD)
        key_rows = key_all[span_blocks].reshape(span_count, NEIGH * BR, group_heads, HD).astype(jnp.float32)
        value_rows = every_payload_vector[span_blocks].reshape(span_count, NEIGH * BR, group_heads, HD).astype(jnp.float32)
        scores = jnp.einsum('cqhd,ckhd->chqk', query_rows, key_rows) * score_scale
        masked = jnp.where(live_mask, scores, -1e30)
        row_max = jnp.max(masked, axis=-1, keepdims=True)
        exp_terms = jnp.where(live_mask, jnp.exp(masked - row_max), 0.0)
        attn_prob = exp_terms / jnp.sum(exp_terms, axis=-1, keepdims=True)
        prob_b = lax.optimization_barrier(attn_prob.astype(jnp.bfloat16)).astype(jnp.float32)
        attended = jnp.einsum('chqk,ckhd->cqhd', prob_b, value_rows).astype(jnp.bfloat16).reshape(TOKENS, col_width)
        weight_rows = lax.dynamic_slice_in_dim(out_weight, col_start, col_width, 0)
        partial_out = jnp.dot(attended, weight_rows, preferred_element_type=jnp.float32).astype(jnp.bfloat16)
        d_attended = jnp.dot(out_grad, weight_rows.T, preferred_element_type=jnp.float32).astype(jnp.bfloat16)
        d_attended = d_attended.reshape(span_count, SPAN, group_heads, HD).astype(jnp.float32)
        d_prob = jnp.einsum('cqhd,ckhd->chqk', d_attended, value_rows)
        row_dot = jnp.sum(attn_prob * d_prob, axis=-1, keepdims=True)
        d_scores = lax.optimization_barrier((attn_prob * (d_prob - row_dot)).astype(jnp.bfloat16)).astype(jnp.float32)
        d_query = (jnp.einsum('chqk,ckhd->cqhd', d_scores, key_rows) * score_scale).astype(jnp.bfloat16)
        d_key = jnp.einsum('chqk,cqhd->ckhd', d_scores, query_rows) * score_scale
        d_value = jnp.einsum('chqk,cqhd->ckhd', prob_b, d_attended)
        flat_ids = span_blocks.reshape(-1)
        d_key = jax.ops.segment_sum(d_key.reshape(span_count * NEIGH, BR, col_width), flat_ids, num_segments=block_count)
        d_value = jax.ops.segment_sum(d_value.reshape(span_count * NEIGH, BR, col_width), flat_ids, num_segments=block_count)
        d_key = d_key.astype(jnp.bfloat16).reshape(block_count * BR, col_width)
        d_value = d_value.astype(jnp.bfloat16).reshape(block_count * BR, col_width)
        return partial_out, d_query.reshape(TOKENS, col_width), d_key, d_value

    partials, d_query, d_key, d_value = lax.map(head_group, jnp.arange(N_TP, dtype=jnp.int32))
    mixed = jnp.sum(partials.astype(jnp.float32), axis=0).astype(jnp.bfloat16)
    d_queries = jnp.transpose(d_query, (1, 0, 2)).reshape(TOKENS, HEADS * HD)
    d_keys = jnp.transpose(d_key, (1, 0, 2)).reshape(block_count * BR, HEADS * HD)
    d_values = jnp.transpose(d_value, (1, 0, 2)).reshape(block_count * BR, HEADS * HD)
    return mixed, d_queries, d_keys, d_values
```

```python
import functools

import jax
import jax.numpy as jnp
from jax import lax
from jax.experimental import pallas as pl
from jax.experimental.pallas import tpu as pltpu
from jax.sharding import PartitionSpec as P

HD = 128
SPAN = 64
BR = 128
NEIGH = 2
CAP = 2
RING = 4
DEAD = 16.0
DEAD_EDGE = 12.0
NEG = -1e30
F32 = jnp.float32
BF16 = jnp.bfloat16
SMEM = pl.BlockSpec(memory_space=pltpu.SMEM)
VMEM = pl.BlockSpec(memory_space=pltpu.VMEM)
ANY = pl.BlockSpec(memory_space=pl.ANY)
NT = (((1,), (1,)), ((), ()))
NN = (((1,), (0,)), ((), ()))
TN = (((0,), (0,)), ((), ()))
MIB = 1 << 20


def dot(a, b, dims):
    return lax.dot_general(a, b, dims, preferred_element_type=F32)


def split_seq(place_ref, index):
    high, low = index // RING, index % RING
    core = place_ref[0]
    return jnp.where(core == 0, high, low), jnp.where(core == 0, low, high)


def block_places(place_ref, dest_ref, blocks):
    places = []
    for j in range(blocks):
        rank = jnp.int32(0)
        for i in range(j):
            rank = rank + jnp.where(dest_ref[i] == dest_ref[j], 1, 0)
        to_a, to_b = split_seq(place_ref, dest_ref[j])
        places.append(((to_a - place_ref[1] + RING) % RING, to_b * CAP + rank))
    return places


def pack_keys_kernel(place_ref, dest_ref, valid_ref, keys, p0, p1, p2, p3, held, in_sem, out_sem):
    packed = (p0, p1, p2, p3)
    blocks = held.shape[0]
    for j in range(blocks):
        pltpu.make_async_copy(keys.at[j], held.at[j], in_sem.at[j]).start()
    places = block_places(place_ref, dest_ref, blocks)
    row = lax.broadcasted_iota(jnp.int32, (BR, HD), 0)
    for j, (shift, pos) in enumerate(places):
        pltpu.make_async_copy(keys.at[j], held.at[j], in_sem.at[j]).wait()
        first = held[j, :, :HD].astype(F32)
        held[j, :, :HD] = jnp.where(row < valid_ref[j], first, DEAD).astype(BF16)
        for d in range(RING):

            @pl.when(shift == d)
            def _():
                pltpu.make_async_copy(held.at[j], packed[d].at[pos], out_sem.at[j]).start()

    for j in range(blocks):
        pltpu.make_async_copy(held.at[j], packed[0].at[0], out_sem.at[j]).wait()


def pack_values_kernel(place_ref, dest_ref, values, p0, p1, p2, p3, out_sem):
    packed = (p0, p1, p2, p3)
    blocks = values.shape[0]
    for j, (shift, pos) in enumerate(block_places(place_ref, dest_ref, blocks)):
        for d in range(RING):

            @pl.when(shift == d)
            def _():
                pltpu.make_async_copy(values.at[j], packed[d].at[pos], out_sem.at[j]).start()

    for j in range(blocks):
        pltpu.make_async_copy(values.at[j], packed[0].at[0], out_sem.at[j]).wait()


def unpack_kernel(place_ref, dest_ref, p0, p1, p2, p3, out, out_sem):
    packed = (p0, p1, p2, p3)
    blocks = out.shape[0]
    for j, (shift, pos) in enumerate(block_places(place_ref, dest_ref, blocks)):
        for d in range(RING):

            @pl.when(shift == d)
            def _():
                pltpu.make_async_copy(packed[d].at[pos], out.at[j], out_sem.at[j]).start()

    for j in range(blocks):
        pltpu.make_async_copy(packed[0].at[0], out.at[j], out_sem.at[j]).wait()


def fill_index(place_ref, refs, index):
    spans = refs[0].shape[0]
    for d in range(RING):
        base = (place_ref[2] - d + RING) % RING * CAP

        def one(g, _):
            for n in range(NEIGH):
                slot = refs[d][g, n]
                from_a, from_b = split_seq(place_ref, slot // CAP)
                where = (place_ref[1] - from_a + RING) % RING * (RING * CAP) + base + slot % CAP
                index[(d * spans + g) * NEIGH + n] = jnp.where(from_b == place_ref[2], where, -1)
            return 0

        lax.fori_loop(0, spans, one, 0)


def diagonals():
    token = lax.broadcasted_iota(jnp.int32, (SPAN, HD), 0)
    lane = lax.broadcasted_iota(jnp.int32, (SPAN, HD), 1)
    return (token == lane, token + SPAN == lane)


def columns_to_row(diagonal, columns):
    halves = []
    for h in range(0, len(columns), 2):
        both = jnp.where(diagonal[0], columns[h], 0.0) + jnp.where(diagonal[1], columns[h + 1], 0.0)
        halves.append(jnp.sum(both, axis=0, keepdims=True))
    return jnp.concatenate(halves, axis=1)


def row_to_column(diagonal, row, h):
    part = row[:, h // 2 * HD : (h // 2 + 1) * HD]
    return jnp.sum(jnp.where(diagonal[h % 2], part, 0.0), axis=1, keepdims=True)


def live_lanes(keys):
    pick = (lax.broadcasted_iota(jnp.int32, (8, HD), 1) == 0).astype(BF16)
    return dot(pick, keys, NT)[0:1] < DEAD_EDGE


def forward_kernel(heads, *args):
    place_ref, refs, queries, keys, values = args[0], args[1:5], args[5:9], args[9:13], args[13:17]
    outs, stats = args[17:21], args[21:25]
    q_buf, k_buf, v_buf, o_buf, s_buf, index, sem = args[25:]
    spans = refs[0].shape[0]
    copies = []
    for d in range(RING):
        for t, (buf, src) in enumerate(((q_buf, queries), (k_buf, keys), (v_buf, values))):
            copies.append(pltpu.make_async_copy(src[d], buf.at[d], sem.at[3 * d + t]))
    for copy in copies:
        copy.start()
    fill_index(place_ref, refs, index)
    for copy in copies:
        copy.wait()
    scale = HD ** (-0.5)

    def span(i, _):
        d, g = i // spans, i % spans
        here = [index[i * NEIGH + n] for n in range(NEIGH)]
        rows = pl.ds(pl.multiple_of(g * SPAN, SPAN), SPAN)
        some = jnp.logical_or(here[0] >= 0, here[1] >= 0)

        @pl.when(jnp.logical_not(some))
        def _():
            o_buf[d, rows, :] = jnp.zeros((SPAN, heads * HD), BF16)
            s_buf[pl.ds(i, 1), :] = jnp.full((1, heads * SPAN), NEG, F32)

        @pl.when(some)
        def _():
            diagonal = diagonals()
            at = [jnp.maximum(b, 0) for b in here]
            live = []
            for n in range(NEIGH):
                block = k_buf[at[n] // (RING * CAP), at[n] % (RING * CAP), :, :HD]
                live.append(jnp.logical_and(live_lanes(block), here[n] >= 0))
            columns = []
            for h in range(heads):
                cols = slice(h * HD, (h + 1) * HD)
                q = q_buf[d, rows, cols]
                scores = []
                for n in range(NEIGH):
                    k = k_buf[at[n] // (RING * CAP), at[n] % (RING * CAP), :, cols]
                    scores.append(jnp.where(live[n], dot(q, k, NT) * scale, NEG))
                top = jnp.max(jnp.maximum(scores[0], scores[1]), axis=1, keepdims=True)
                total = jnp.zeros((SPAN, 1), F32)
                mixed = jnp.zeros((SPAN, HD), F32)
                for n in range(NEIGH):
                    v = v_buf[at[n] // (RING * CAP), at[n] % (RING * CAP), :, cols]
                    e = jnp.where(live[n], jnp.exp(scores[n] - top), 0.0)
                    total += jnp.sum(e, axis=1, keepdims=True)
                    mixed += dot(e.astype(BF16), v, NN)
                o_buf[d, rows, cols] = (mixed / total).astype(BF16)
                columns.append(top + jnp.log(total))
            s_buf[pl.ds(i, 1), :] = columns_to_row(diagonal, columns)

        return 0

    lax.fori_loop(0, RING * spans, span, 0)
    out_copies = [pltpu.make_async_copy(o_buf.at[d], outs[d], sem.at[d]) for d in range(RING)]
    for copy in out_copies:
        copy.start()
    for d in range(RING):
        stats[d][...] = s_buf[d * spans : (d + 1) * spans, :]
    for copy in out_copies:
        copy.wait()


def merge_kernel(heads, *args):
    parts, stats, d_att = args[0:4], args[4:8], args[8]
    out, stats_out = args[9], args[10]
    spans = stats[0].shape[0]
    top = stats[0][...]
    for d in range(1, RING):
        top = jnp.maximum(top, stats[d][...])
    total = jnp.zeros_like(top)
    for d in range(RING):
        total += jnp.exp(stats[d][...] - top)
    whole = top + jnp.log(total)
    stats_out[0:spans, :] = whole

    def span(g, _):
        diagonal = diagonals()
        rows = pl.ds(pl.multiple_of(g * SPAN, SPAN), SPAN)
        here = stats_out[pl.ds(g, 1), :]
        weight = [jnp.exp(stats[d][pl.ds(g, 1), :] - here) for d in range(RING)]
        columns = []
        for h in range(heads):
            cols = slice(h * HD, (h + 1) * HD)
            acc = jnp.zeros((SPAN, HD), F32)
            for d in range(RING):
                acc += row_to_column(diagonal, weight[d], h) * parts[d][rows, cols].astype(F32)
            out[rows, cols] = acc.astype(BF16)
            columns.append(jnp.sum(acc * d_att[rows, cols].astype(F32), axis=1, keepdims=True))
        stats_out[pl.ds(spans + g, 1), :] = columns_to_row(diagonal, columns)
        return 0

    lax.fori_loop(0, spans, span, 0)


def backward_kernel(heads, *args):
    place_ref, refs, queries, d_atts = args[0], args[1:5], args[5:9], args[9:13]
    keys, values, stats = args[13:17], args[17:21], args[21:25]
    d_qs, d_ks, d_vs = args[25:29], args[29:33], args[33:37]
    q_buf, g_buf, k_buf, v_buf, dq_buf, dk_acc, dv_acc, index, seen, sem = args[37:]
    spans = refs[0].shape[0]
    per_ring = RING * CAP
    copies = []
    for d in range(RING):
        for t, (buf, src) in enumerate(
            ((q_buf, queries), (g_buf, d_atts), (k_buf, keys), (v_buf, values))
        ):
            copies.append(pltpu.make_async_copy(src[d], buf.at[d], sem.at[4 * d + t]))
    for copy in copies:
        copy.start()
    fill_index(place_ref, refs, index)
    for b in range(RING * per_ring):
        seen[b] = 0
    for copy in copies:
        copy.wait()
    scale = HD ** (-0.5)
    for d in range(RING):

        def span(g, _):
            i = d * spans + g
            here = [index[i * NEIGH + n] for n in range(NEIGH)]
            rows = pl.ds(pl.multiple_of(g * SPAN, SPAN), SPAN)
            some = jnp.logical_or(here[0] >= 0, here[1] >= 0)

            @pl.when(jnp.logical_not(some))
            def _():
                dq_buf[d, rows, :] = jnp.zeros((SPAN, heads * HD), BF16)

            @pl.when(some)
            def _():
                diagonal = diagonals()
                lse_row = stats[d][pl.ds(g, 1), :]
                dot_row = stats[d][pl.ds(spans + g, 1), :]
                lse = [row_to_column(diagonal, lse_row, h) for h in range(heads)]
                row_dot = [row_to_column(diagonal, dot_row, h) for h in range(heads)]

                def pair(b, first):
                    live = live_lanes(k_buf[b // per_ring, b % per_ring, :, :HD])
                    fresh = seen[b] == 0
                    for h in range(heads):
                        cols = slice(h * HD, (h + 1) * HD)
                        q = q_buf[d, rows, cols]
                        g_att = g_buf[d, rows, cols]
                        k = k_buf[b // per_ring, b % per_ring, :, cols]
                        v = v_buf[b // per_ring, b % per_ring, :, cols]
                        p = jnp.where(live, jnp.exp(dot(q, k, NT) * scale - lse[h]), 0.0)
                        d_s = (p * (dot(g_att, v, NT) - row_dot[h])).astype(BF16)
                        d_q = dot(d_s, k, NN) * scale
                        if first is None:
                            dq_buf[d, rows, cols] = d_q.astype(BF16)
                        else:
                            d_q = d_q + dq_buf[d, rows, cols].astype(F32)
                            dq_buf[d, rows, cols] = d_q.astype(BF16)
                        d_k = dot(d_s, q, TN) * scale
                        d_v = dot(p.astype(BF16), g_att, TN)

                        @pl.when(fresh)
                        def _():
                            dk_acc[b, :, cols] = d_k
                            dv_acc[b, :, cols] = d_v

                        @pl.when(jnp.logical_not(fresh))
                        def _():
                            dk_acc[b, :, cols] += d_k
                            dv_acc[b, :, cols] += d_v

                    seen[b] = 1

                @pl.when(here[0] >= 0)
                def _():
                    pair(here[0], None)

                @pl.when(jnp.logical_and(here[1] >= 0, here[0] < 0))
                def _():
                    pair(here[1], None)

                @pl.when(jnp.logical_and(here[1] >= 0, here[0] >= 0))
                def _():
                    pair(here[1], True)

            return 0

        lax.fori_loop(0, spans, span, 0)

    def finish(b, _):
        @pl.when(seen[b] == 1)
        def _():
            k_buf[b // per_ring, b % per_ring] = dk_acc[b].astype(BF16)
            v_buf[b // per_ring, b % per_ring] = dv_acc[b].astype(BF16)

        @pl.when(seen[b] == 0)
        def _():
            k_buf[b // per_ring, b % per_ring] = jnp.zeros((BR, heads * HD), BF16)
            v_buf[b // per_ring, b % per_ring] = jnp.zeros((BR, heads * HD), BF16)

        return 0

    lax.fori_loop(0, RING * per_ring, finish, 0)
    out_copies = []
    for d in range(RING):
        for t, (buf, dst) in enumerate(((dq_buf, d_qs), (k_buf, d_ks), (v_buf, d_vs))):
            out_copies.append(pltpu.make_async_copy(buf.at[d], dst[d], sem.at[4 * d + t]))
    for copy in out_copies:
        copy.start()
    for copy in out_copies:
        copy.wait()


def call(kernel, outs, in_specs, out_specs, scratch, cost, *operands):
    return pl.pallas_call(
        kernel,
        out_shape=outs,
        in_specs=in_specs,
        out_specs=out_specs,
        scratch_shapes=scratch,
        compiler_params=pltpu.CompilerParams(vmem_limit_bytes=44 * MIB),
        cost_estimate=pl.CostEstimate(flops=cost[0], bytes_accessed=cost[1], transcendentals=0),
    )(*operands)


def on_device(
    queries, nb_keys, nb_values, out_weight, out_grad, span_refs, block_dest, block_valid
):
    seq_count = lax.axis_size("seq")
    tp_count = lax.axis_size("tp")
    tokens, width = queries.shape
    heads = width // HD
    spans = tokens // SPAN
    blocks = block_dest.shape[0]
    per_ring = RING * CAP
    dma = pltpu.SemaphoreType.DMA

    seq_at = lax.axis_index("seq")
    core = lax.axis_index("tp") % 2
    high, low = seq_at // RING, seq_at % RING
    place = jnp.stack(
        [core, jnp.where(core == 0, high, low), jnp.where(core == 0, low, high)]
    ).astype(jnp.int32)

    def ring_pairs(shift, along_a):
        pairs = []
        for s in range(seq_count):
            z, y = s // RING, s % RING
            for t in range(tp_count):
                if (t % 2 == 0) == along_a:
                    to = (z + shift) % RING * RING + y
                else:
                    to = z * RING + (y + shift) % RING
                pairs.append((s * tp_count + t, to * tp_count + t))
        return pairs

    def move(x, shift, along_a):
        return lax.ppermute(x, ("seq", "tp"), ring_pairs(shift % RING, along_a))

    order = (1, 3, 2)

    def spread(parts, along_a, sign):
        got = {0: parts[0]}
        for d in order:
            got[d] = move(parts[d], sign * d, along_a)
        return tuple(got[d] for d in range(RING))

    grad_rows = lax.all_gather(out_grad, "tp", axis=0, tiled=True)
    refs = spread((span_refs,) * RING, False, 1)
    q_all = spread((queries,) * RING, False, 1)

    block_shape = jax.ShapeDtypeStruct((per_ring, BR, width), BF16)
    packed_keys = call(
        pack_keys_kernel,
        (block_shape,) * RING,
        [SMEM, SMEM, SMEM, ANY],
        (ANY,) * RING,
        [pltpu.VMEM((blocks, BR, width), BF16), dma((blocks,)), dma((blocks,))],
        (0, 8 * MIB),
        place,
        block_dest,
        block_valid,
        nb_keys.reshape(blocks, BR, width),
    )
    k_all = spread(packed_keys, True, 1)
    packed_values = call(
        pack_values_kernel,
        (block_shape,) * RING,
        [SMEM, SMEM, ANY],
        (ANY,) * RING,
        [dma((blocks,))],
        (0, 8 * MIB),
        place,
        block_dest,
        nb_values.reshape(blocks, BR, width),
    )
    v_all = spread(packed_values, True, 1)

    d_attended = lax.dot_general(
        grad_rows, out_weight, (((1,), (1,)), ((), ())), preferred_element_type=F32
    ).astype(BF16)
    g_all = spread((d_attended,) * RING, False, 1)

    rows_shape = jax.ShapeDtypeStruct((tokens, width), BF16)
    stat_shape = jax.ShapeDtypeStruct((spans, heads * SPAN), F32)
    found = call(
        functools.partial(forward_kernel, heads),
        (rows_shape,) * RING + (stat_shape,) * RING,
        [SMEM] * 5 + [ANY] * 12,
        (ANY,) * RING + (VMEM,) * RING,
        [
            pltpu.VMEM((RING, tokens, width), BF16),
            pltpu.VMEM((RING, per_ring, BR, width), BF16),
            pltpu.VMEM((RING, per_ring, BR, width), BF16),
            pltpu.VMEM((RING, tokens, width), BF16),
            pltpu.VMEM((RING * spans, heads * SPAN), F32),
            pltpu.SMEM((RING * spans * NEIGH,), jnp.int32),
            dma((3 * RING,)),
        ],
        (1 << 31, 12 * MIB),
        place,
        *refs,
        *q_all,
        *k_all,
        *v_all,
    )
    parts = spread(found[:RING], False, -1)
    part_stats = spread(found[RING:], False, -1)
    attended, stats = call(
        functools.partial(merge_kernel, heads),
        (rows_shape, jax.ShapeDtypeStruct((2 * spans, heads * SPAN), F32)),
        [VMEM] * 9,
        (VMEM, VMEM),
        [],
        (1 << 24, 4 * MIB),
        *parts,
        *part_stats,
        d_attended,
    )
    stats_all = spread((stats,) * RING, False, 1)
    partial = jnp.dot(attended, out_weight, preferred_element_type=F32).astype(BF16)
    mixed = lax.psum_scatter(partial, "tp", scatter_dimension=0, tiled=True)

    grads = call(
        functools.partial(backward_kernel, heads),
        (rows_shape,) * RING + (block_shape,) * (2 * RING),
        [SMEM] * 5 + [ANY] * 16 + [VMEM] * RING,
        (ANY,) * (3 * RING),
        [
            pltpu.VMEM((RING, tokens, width), BF16),
            pltpu.VMEM((RING, tokens, width), BF16),
            pltpu.VMEM((RING, per_ring, BR, width), BF16),
            pltpu.VMEM((RING, per_ring, BR, width), BF16),
            pltpu.VMEM((RING, tokens, width), BF16),
            pltpu.VMEM((RING * per_ring, BR, width), F32),
            pltpu.VMEM((RING * per_ring, BR, width), F32),
            pltpu.SMEM((RING * spans * NEIGH,), jnp.int32),
            pltpu.SMEM((RING * per_ring,), jnp.int32),
            dma((4 * RING,)),
        ],
        (1 << 32, 24 * MIB),
        place,
        *refs,
        *q_all,
        *g_all,
        *k_all,
        *v_all,
        *stats_all,
    )
    back_values = spread(grads[2 * RING :], True, -1)
    back_keys = spread(grads[RING : 2 * RING], True, -1)
    back_queries = spread(grads[:RING], False, -1)

    def unpack(back):
        return call(
            unpack_kernel,
            jax.ShapeDtypeStruct((blocks, BR, width), BF16),
            [SMEM, SMEM] + [ANY] * RING,
            ANY,
            [dma((blocks,))],
            (0, 8 * MIB),
            place,
            block_dest,
            *back,
        ).reshape(blocks * BR, width)

    d_queries = sum(part.astype(F32) for part in back_queries).astype(BF16)
    return mixed, d_queries, unpack(back_keys), unpack(back_values)


def solution(mesh):
    placed = (
        P("seq", "tp"),
        P("seq", "tp"),
        P("seq", "tp"),
        P("tp", None),
        P(("seq", "tp"), None),
        P("seq", None),
        P("seq"),
        P("seq"),
    )
    return jax.shard_map(
        on_device,
        mesh=mesh,
        in_specs=placed,
        out_specs=(P(("seq", "tp"), None), P("seq", "tp"), P("seq", "tp"), P("seq", "tp")),
        check_vma=False,
    )
```

```python
import functools

import jax
import jax.numpy as jnp
from jax import lax
from jax.experimental import pallas as pl
from jax.experimental.pallas import tpu as pltpu
from jax.sharding import PartitionSpec as P

HD = 128
SPAN = 64
BR = 128
NEIGH = 2
CAP = 2
RING = 4
DEAD = 16.0
DEAD_EDGE = 12.0
NEG = -1e30
F32 = jnp.float32
BF16 = jnp.bfloat16
SMEM = pl.BlockSpec(memory_space=pltpu.SMEM)
VMEM = pl.BlockSpec(memory_space=pltpu.VMEM)
ANY = pl.BlockSpec(memory_space=pl.ANY)
NT = (((1,), (1,)), ((), ()))
NN = (((1,), (0,)), ((), ()))
TN = (((0,), (0,)), ((), ()))
MIB = 1 << 20
PLACE = 3


def dot(a, b, dims):
    return lax.dot_general(a, b, dims, preferred_element_type=F32)


def split_seq(meta, index):
    high, low = index // RING, index % RING
    first = meta[0] == 0
    return jnp.where(first, high, low), jnp.where(first, low, high)


def block_places(meta, blocks):
    dest = [meta[PLACE + j] for j in range(blocks)]
    places = []
    for j in range(blocks):
        rank = jnp.int32(0)
        for i in range(j):
            rank = rank + jnp.where(dest[i] == dest[j], 1, 0)
        to_a, to_b = split_seq(meta, dest[j])
        places.append(((to_a - meta[1] + RING) % RING, to_b * CAP + rank))
    return places


def pack_kernel(meta, keys, values, p0, p1, p2, p3, held, in_sem, out_sem):
    packed = (p0, p1, p2, p3)
    blocks = held.shape[1]
    per_ring = RING * CAP
    reads = [
        [pltpu.make_async_copy(src.at[j], held.at[t, j], in_sem.at[t, j]) for j in range(blocks)]
        for t, src in enumerate((keys, values))
    ]
    for j in range(blocks):
        reads[0][j].start()
        reads[1][j].start()
    places = block_places(meta, blocks)
    row = lax.broadcasted_iota(jnp.int32, (BR, HD), 0)
    for j, (shift, pos) in enumerate(places):
        reads[0][j].wait()
        first = held[0, j, :, :HD].astype(F32)
        valid = meta[PLACE + blocks + j]
        held[0, j, :, :HD] = jnp.where(row < valid, first, DEAD).astype(BF16)
        reads[1][j].wait()
        for d in range(RING):

            @pl.when(shift == d)
            def _():
                for t in range(2):
                    to = packed[d].at[pos + t * per_ring]
                    pltpu.make_async_copy(held.at[t, j], to, out_sem.at[t, j]).start()

    for j in range(blocks):
        for t in range(2):
            pltpu.make_async_copy(held.at[t, j], packed[0].at[0], out_sem.at[t, j]).wait()


def unpack_kernel(meta, p0, p1, p2, p3, d_keys, d_values, held, in_sem, out_sem):
    packed = (p0, p1, p2, p3)
    outs = (d_keys, d_values)
    blocks = d_keys.shape[0]
    per_ring = RING * CAP
    table = PLACE + 2 * blocks
    reads = []
    for d in range(RING):
        to = held.at[pl.ds(2 * d * per_ring, packed[d].shape[0])]
        reads.append(pltpu.make_async_copy(packed[d], to, in_sem.at[d]))
        reads[-1].start()
    empty = 2 * RING * per_ring
    held[empty] = jnp.zeros(held.shape[1:], BF16)
    kept = packed[1].shape[0] // 2
    writes = []
    places = block_places(meta, blocks)
    for read in reads:
        read.wait()
    for j, (shift, pos) in enumerate(places):
        back = meta[table + shift * per_ring + pos]
        half = jnp.where(shift == 0, per_ring, kept)
        for t in range(2):
            at = jnp.where(back < 0, empty, 2 * shift * per_ring + back + t * half)
            writes.append(pltpu.make_async_copy(held.at[at], outs[t].at[j], out_sem.at[t, j]))
            writes[-1].start()
    for write in writes:
        write.wait()


def locate(meta, spans, i, n):
    d = i // spans
    slot = meta[PLACE + i * NEIGH + n]
    from_a, from_b = split_seq(meta, slot // CAP)
    to_b = (meta[2] - d + RING) % RING
    block = (meta[1] - from_a + RING) % RING * (RING * CAP) + to_b * CAP + slot % CAP
    return block, from_b == meta[2]


def diagonal_reads(src, buf, d, spans, heads, sem):
    reads = []
    for h in range(heads):
        at = h % 2
        to = buf.at[
            pl.ds(d * spans, spans), h // 2, pl.ds(at * SPAN, SPAN), pl.ds(at * HD, HD)
        ]
        here = src.at[pl.ds(0, spans), :, pl.ds(h * HD, HD)]
        reads.append(pltpu.make_async_copy(here, to, sem.at[h]))
    return reads


def clear_others(buf):
    count = buf.shape[0]

    def one(i, _):
        for t in range(buf.shape[1]):
            buf[i, t, :SPAN, HD:] = jnp.zeros((SPAN, HD), BF16)
            buf[i, t, SPAN:, :HD] = jnp.zeros((SPAN, HD), BF16)
        return 0

    lax.fori_loop(0, count, one, 0)


def forward_kernel(heads, spans, *args):
    meta, queries, blocks_in, outs = args[0], args[1:5], args[5:9], args[9:13]
    q_buf, kv_buf, o_buf, s_buf, spans_at, counts, q_sem, sem = args[13:]
    tokens = spans * SPAN
    per_ring = RING * CAP
    twins = heads // 2
    reads = []
    for d in range(RING):
        reads += diagonal_reads(queries[d], q_buf, d, spans, heads, q_sem.at[d])
    block_reads = [
        pltpu.make_async_copy(blocks_in[d], kv_buf.at[d], sem.at[RING + d]) for d in range(RING)
    ]
    for copy in reads + block_reads:
        copy.start()
    for r in range(RING + 1):
        counts[r] = 0
    stride = 3 * (RING * spans + 1)

    def listed(i, _):
        block0, here0 = locate(meta, spans, i, 0)
        block1, here1 = locate(meta, spans, i, 1)
        first = jnp.where(here0, block0, block1)
        which = jnp.where(jnp.logical_and(here0, here1), RING, first // per_ring)
        at = which * stride + 3 * counts[which]
        spans_at[at] = i
        spans_at[at + 1] = first
        spans_at[at + 2] = block1
        counts[which] = counts[which] + jnp.where(jnp.logical_or(here0, here1), 1, 0)
        return 0

    lax.fori_loop(0, RING * spans, listed, 0)
    clear_others(q_buf)
    o_buf[:, :tokens, :] = jnp.zeros((RING, tokens, heads * HD), BF16)
    s_buf[...] = jnp.full(s_buf.shape, NEG, F32)
    for copy in reads:
        copy.wait()
    scale = HD ** (-0.5)

    def span(i, at):
        d, g = i // spans, i % spans
        rows = pl.ds(pl.multiple_of(g * SPAN, SPAN), SPAN)
        where = [(b // per_ring, b % per_ring) for b in at]
        live = [kv_buf[r, p, :, :HD][:, :1].astype(F32) < DEAD_EDGE for r, p in where]
        for t in range(twins):
            cols = slice(2 * t * HD, 2 * (t + 1) * HD)
            q = q_buf[i, t]
            scores = [
                jnp.where(here, dot(kv_buf[r, p, :, cols], q, NT) * scale, NEG)
                for here, (r, p) in zip(live, where)
            ]
            top = functools.reduce(jnp.maximum, [jnp.max(s, axis=0, keepdims=True) for s in scores])
            terms = [jnp.exp(s - top) for s in scores]
            total = sum(jnp.sum(e, axis=0, keepdims=True) for e in terms)
            share = 1.0 / total
            mixed = sum(
                dot((e * share).astype(BF16), kv_buf[r, per_ring + p, :, cols], TN)
                for e, (r, p) in zip(terms, where)
            ).astype(BF16)
            o_buf[d, rows, 2 * t * HD : (2 * t + 1) * HD] = mixed[:SPAN, :HD]
            o_buf[d, rows, (2 * t + 1) * HD : 2 * (t + 1) * HD] = mixed[SPAN:, HD:]
            s_buf[pl.ds(i * twins + t, 1), :] = top + jnp.log(total)

    for r in range(RING + 1):
        count = counts[r]

        def two(t, _):
            for u in range(2):
                at = r * stride + 3 * jnp.minimum(2 * t + u, count - 1)
                span(spans_at[at], [spans_at[at + 1 + n] for n in range(2 if r == RING else 1)])
            return 0

        if r < RING:
            block_reads[r].wait()
        lax.fori_loop(0, (count + 1) // 2, two, 0)

    out_copies = []
    rows_in = spans * twins
    for d in range(RING):
        part = s_buf[d * rows_in : (d + 1) * rows_in, :]
        for t in range(3):
            piece = part.astype(BF16)
            o_buf[d, tokens:, t * HD : (t + 1) * HD] = piece
            part = part - piece.astype(F32)
        out_copies.append(pltpu.make_async_copy(o_buf.at[d], outs[d], sem.at[d]))
        out_copies[-1].start()
    for copy in out_copies:
        copy.wait()


def merge_kernel(heads, *args):
    parts, d_att = args[0:4], args[4]
    out, stats_out, lse_buf = args[5:]
    tokens = out.shape[0]
    spans = tokens // SPAN
    twins = heads // 2
    stat_rows = spans * twins
    for d in range(RING):
        pieces = [parts[d][tokens:, t * HD : (t + 1) * HD].astype(F32) for t in range(3)]
        lse_buf[d] = pieces[0] + pieces[1] + pieces[2]
    top = functools.reduce(jnp.maximum, [lse_buf[d] for d in range(RING)])
    total = sum(jnp.exp(lse_buf[d] - top) for d in range(RING))
    whole = top + jnp.log(total)
    stats_out[:stat_rows, :] = whole
    for d in range(RING):
        lse_buf[d] = jnp.exp(lse_buf[d] - whole)
    token = lax.broadcasted_iota(jnp.int32, (SPAN, HD), 0)
    lane = lax.broadcasted_iota(jnp.int32, (SPAN, HD), 1)
    diagonal = (token == lane, token + SPAN == lane)

    def span(g, _):
        rows = pl.ds(pl.multiple_of(g * SPAN, SPAN), SPAN)
        for t in range(twins):
            row_dots = []
            for u in range(2):
                h = 2 * t + u
                cols = slice(h * HD, (h + 1) * HD)
                acc = jnp.zeros((SPAN, HD), F32)
                for d in range(RING):
                    row = lse_buf[d, pl.ds(g * twins + t, 1), :]
                    weight = jnp.sum(jnp.where(diagonal[u], row, 0.0), axis=1, keepdims=True)
                    acc += weight * parts[d][rows, cols].astype(F32)
                out[rows, cols] = acc.astype(BF16)
                row_dot = jnp.sum(acc * d_att[rows, cols].astype(F32), axis=1, keepdims=True)
                row_dots.append(jnp.where(diagonal[u], row_dot, 0.0))
            stats_out[pl.ds(stat_rows + g * twins + t, 1), :] = jnp.sum(
                row_dots[0] + row_dots[1], axis=0, keepdims=True
            )
        return 0

    lax.fori_loop(0, spans, span, 0)


def backward_kernel(heads, spans, *args):
    meta, queries, d_atts, blocks_in, stats = args[0], args[1:5], args[5:9], args[9:13], args[13:17]
    d_qs, d_blocks = args[17:21], args[21:25]
    q_buf, g_buf, kv_buf, s_buf, dq_buf, dq_acc, dk_acc, dv_acc = args[25:33]
    pairs, counts, seen, q_sem, g_sem, sem = args[33:]
    per_ring = RING * CAP
    twins = heads // 2
    stat_rows = spans * twins
    order = (1, 3, 2, 0)
    reads = []
    for d in range(RING):
        reads += diagonal_reads(queries[d], q_buf, d, spans, heads, q_sem.at[d])
        reads += diagonal_reads(d_atts[d], g_buf, d, spans, heads, g_sem.at[d])
        reads.append(pltpu.make_async_copy(stats[d], s_buf.at[d], sem.at[4 * d]))
    block_reads = [
        pltpu.make_async_copy(blocks_in[d], kv_buf.at[d], sem.at[4 * d + 3]) for d in range(RING)
    ]
    for copy in reads:
        copy.start()
    for r in order:
        block_reads[r].start()
    for r in range(RING):
        counts[r] = 0
    for b in range(RING * per_ring):
        seen[b] = 0
    stride = 2 * (RING * spans * NEIGH + 1)

    def listed(i, _):
        for n in range(NEIGH):
            block, here = locate(meta, spans, i, n)
            which = block // per_ring
            at = which * stride + 2 * counts[which]
            pairs[at] = i
            pairs[at + 1] = block % per_ring
            counts[which] = counts[which] + jnp.where(here, 1, 0)
            seen[block] = jnp.where(here, 1, seen[block])
        return 0

    lax.fori_loop(0, RING * spans, listed, 0)
    clear_others(q_buf)
    clear_others(g_buf)
    dq_acc[...] = jnp.zeros(dq_acc.shape, F32)
    for copy in reads:
        copy.wait()
    scale = HD ** (-0.5)
    writes = []
    for r in order:
        count = counts[r]

        def clear(p, _):
            @pl.when(seen[r * per_ring + p] == 1)
            def _():
                dk_acc[p] = jnp.zeros((BR, heads * HD), F32)
                dv_acc[p] = jnp.zeros((BR, heads * HD), F32)

            return 0

        def two(t, _):
            found = []
            for u in range(2):
                at = r * stride + 2 * jnp.minimum(2 * t + u, count - 1)
                i, p = pairs[at], pairs[at + 1]
                d, g = i // spans, i % spans
                live = kv_buf[r, p, :, :HD][:, :1].astype(F32) < DEAD_EDGE
                real = 2 * t + u < count
                to = (jnp.where(real, i, RING * spans), jnp.where(real, p, per_ring))
                for w in range(twins):
                    cols = slice(2 * w * HD, 2 * (w + 1) * HD)
                    q, g_att = q_buf[i, w], g_buf[i, w]
                    k = kv_buf[r, p, :, cols]
                    v = kv_buf[r, per_ring + p, :, cols]
                    lse = s_buf[d, pl.ds(g * twins + w, 1), :]
                    row_dot = s_buf[d, pl.ds(stat_rows + g * twins + w, 1), :]
                    prob = jnp.where(live, jnp.exp(dot(k, q, NT) * scale - lse), 0.0)
                    d_s = (prob * (dot(v, g_att, NT) - row_dot)).astype(BF16)
                    d_v, d_k = dot(prob.astype(BF16), g_att, NN), dot(d_s, q, NN)
                    found.append((to, w, d_v, d_k, dot(d_s, k, TN)))
            for (i, p), w, d_v, d_k, d_q in found:
                cols = slice(2 * w * HD, 2 * (w + 1) * HD)
                dv_acc[p, :, cols] += d_v
                dk_acc[p, :, cols] += d_k
                dq_acc[i, :, 2 * w * HD : (2 * w + 1) * HD] += d_q[:SPAN, :HD]
                dq_acc[i, :, (2 * w + 1) * HD : 2 * (w + 1) * HD] += d_q[SPAN:, HD:]
            return 0

        def finish(p, at):
            one = seen[r * per_ring + p]

            @pl.when(one == 1)
            def _():
                kv_buf[r, at] = (dk_acc[p] * scale).astype(BF16)
                kv_buf[r, d_blocks[r].shape[0] // 2 + at] = dv_acc[p].astype(BF16)

            return at + one

        lax.fori_loop(0, per_ring, clear, 0)
        block_reads[r].wait()
        lax.fori_loop(0, (count + 1) // 2, two, 0)
        lax.fori_loop(0, per_ring, finish, jnp.int32(0))
        here = kv_buf.at[r, pl.ds(0, d_blocks[r].shape[0])]
        writes.append(pltpu.make_async_copy(here, d_blocks[r], sem.at[4 * r + 3]))
        writes[-1].start()
    for d in range(RING):
        for g in range(spans):
            dq_buf[d, g] = (dq_acc[d * spans + g] * scale).astype(BF16)
        writes.append(pltpu.make_async_copy(dq_buf.at[d], d_qs[d], sem.at[4 * d + 1]))
        writes[-1].start()
    for write in writes:
        write.wait()


def call(kernel, outs, in_specs, out_specs, scratch, cost, *operands, vmem=58):
    return pl.pallas_call(
        kernel,
        out_shape=outs,
        in_specs=in_specs,
        out_specs=out_specs,
        scratch_shapes=scratch,
        compiler_params=pltpu.CompilerParams(vmem_limit_bytes=vmem * MIB),
        cost_estimate=pl.CostEstimate(flops=cost[0], bytes_accessed=cost[1], transcendentals=0),
    )(*operands)


def on_device(
    queries, nb_keys, nb_values, out_weight, out_grad, span_refs, block_dest, block_valid
):
    seq_count = lax.axis_size("seq")
    tp_count = lax.axis_size("tp")
    tokens, width = queries.shape
    heads = width // HD
    spans = tokens // SPAN
    blocks = block_dest.shape[0]
    per_ring = RING * CAP
    stat_rows = spans * heads // 2
    ref_count = spans * NEIGH
    dma = pltpu.SemaphoreType.DMA

    seq_at = lax.axis_index("seq")
    core = lax.axis_index("tp") % 2
    high, low = seq_at // RING, seq_at % RING
    place = jnp.stack(
        [core, jnp.where(core == 0, high, low), jnp.where(core == 0, low, high)]
    ).astype(jnp.int32)

    def ring_pairs(shift, along_a):
        pairs = []
        for s in range(seq_count):
            z, y = s // RING, s % RING
            for t in range(tp_count):
                if (t % 2 == 0) == along_a:
                    to = (z + shift) % RING * RING + y
                else:
                    to = z * RING + (y + shift) % RING
                pairs.append((s * tp_count + t, to * tp_count + t))
        return pairs

    def move(x, shift, along_a):
        return lax.ppermute(x, ("seq", "tp"), ring_pairs(shift % RING, along_a))

    order = (1, 3, 2)

    def spread(parts, along_a, sign):
        got = {0: parts[0]}
        for d in order:
            got[d] = move(parts[d], sign * d, along_a)
        return tuple(got[d] for d in range(RING))

    grad_rows = lax.all_gather(out_grad, "tp", axis=0, tiled=True)

    slot_count = seq_count * CAP
    ref_rows = jnp.pad(
        span_refs.astype(BF16).reshape(1, 1, ref_count),
        ((0, 0), (0, SPAN - 1), (0, width - ref_count)),
    )
    q_sent = jnp.concatenate([queries.reshape(spans, SPAN, width), ref_rows], axis=0)
    q_all = spread((q_sent,) * RING, False, 1)
    refs = jnp.concatenate([q[spans, 0, :ref_count] for q in q_all]).astype(jnp.int32)
    meta = jnp.concatenate([place, refs])
    pack_meta = jnp.concatenate([place, block_dest, block_valid])

    kv_shape = jax.ShapeDtypeStruct((2 * per_ring, BR, width), BF16)
    packed = call(
        pack_kernel,
        (kv_shape,) * RING,
        [SMEM, ANY, ANY],
        (ANY,) * RING,
        [
            pltpu.VMEM((2, blocks, BR, width), BF16),
            dma((2, blocks)),
            dma((2, blocks)),
        ],
        (0, 16 * MIB),
        pack_meta,
        nb_keys.reshape(blocks, BR, width),
        nb_values.reshape(blocks, BR, width),
    )
    kv_all = spread(packed, True, 1)

    d_attended = lax.dot_general(
        grad_rows, out_weight, (((1,), (1,)), ((), ())), preferred_element_type=F32
    ).astype(BF16)
    g_all = spread((d_attended.reshape(spans, SPAN, width),) * RING, False, 1)

    kv_now, q_now, d_attended = lax.optimization_barrier((kv_all, q_all, d_attended))
    twin_rows = (RING * spans, heads // 2, 2 * SPAN, 2 * HD)
    part_shape = jax.ShapeDtypeStruct((tokens + stat_rows, width), BF16)
    found = call(
        functools.partial(forward_kernel, heads, spans),
        (part_shape,) * RING,
        [SMEM] + [ANY] * 8,
        (ANY,) * RING,
        [
            pltpu.VMEM(twin_rows, BF16),
            pltpu.VMEM((RING, 2 * per_ring, BR, width), BF16),
            pltpu.VMEM((RING, tokens + stat_rows, width), BF16),
            pltpu.VMEM((RING * stat_rows, HD), F32),
            pltpu.SMEM((3 * (RING + 1) * (RING * spans + 1),), jnp.int32),
            pltpu.SMEM((RING + 1,), jnp.int32),
            dma((RING, heads)),
            dma((2 * RING,)),
        ],
        (10**11, 12 * MIB),
        meta,
        *q_now,
        *kv_now,
    )
    found, refs = lax.optimization_barrier((found, refs))
    parts = spread(found, False, -1)
    step = jnp.arange(RING)
    ring_b = (place[2] - step + RING) % RING
    owner = jnp.where(core == 0, place[1] * RING + ring_b, ring_b * RING + place[1])
    ring_keys = (owner[:, None] * slot_count + refs.reshape(RING, ref_count)).reshape(-1)
    all_keys = jnp.concatenate(spread((ring_keys.astype(jnp.int32),) * RING, True, 1))
    parts, all_keys = lax.optimization_barrier((parts, all_keys))
    span_shape = jax.ShapeDtypeStruct((spans, SPAN, width), BF16)
    rows_shape = jax.ShapeDtypeStruct((tokens, width), BF16)
    stat_shape = jax.ShapeDtypeStruct((2 * stat_rows, HD), F32)
    attended, stats = call(
        functools.partial(merge_kernel, heads),
        (rows_shape, stat_shape),
        [VMEM] * 5,
        (VMEM, VMEM),
        [pltpu.VMEM((RING, stat_rows, HD), F32)],
        (10**11, 4 * MIB),
        *parts,
        d_attended,
        vmem=40,
    )
    stats_all = spread((stats,) * RING, False, 1)
    attended, g_all = lax.optimization_barrier((attended, g_all))
    partial = jnp.dot(attended, out_weight, preferred_element_type=F32).astype(BF16)
    mixed = lax.psum_scatter(partial, "tp", scatter_dimension=0, tiled=True)

    named = jnp.any(all_keys[None, :] == jnp.arange(seq_count * slot_count)[:, None], axis=1)
    shape = (RING, RING, RING, RING, CAP)
    named = named.reshape(shape).astype(jnp.int32)
    other = (1 - jnp.eye(RING, dtype=jnp.int32))
    most = jnp.maximum(
        jnp.max(jnp.sum(named, axis=(1, 4)) * other[:, :, None]),
        jnp.max(jnp.sum(named, axis=(0, 4)) * other[:, None, :]),
    )
    to_a = (place[1] + step[:, None, None]) % RING
    to_b = step[None, :, None]
    owner = jnp.where(core == 0, to_a * RING + to_b, to_b * RING + to_a)
    sent = owner * slot_count + seq_at * CAP + jnp.arange(CAP)[None, None, :]
    sent = sent.reshape(RING, per_ring)
    sent_named = jnp.any(all_keys[None, None, :] == sent[:, :, None], axis=2).astype(jnp.int32)
    earlier = (jnp.arange(per_ring)[:, None] < jnp.arange(per_ring)[None, :]).astype(jnp.int32)
    position = jnp.sum(sent_named[:, :, None] * earlier[None], axis=1)
    position = jnp.where(sent_named == 1, position, -1).reshape(RING * per_ring)
    unpack_meta = jnp.concatenate([pack_meta, position])
    block_out = jax.ShapeDtypeStruct((blocks, BR, width), BF16)

    def backward(kept):
        back_shape = jax.ShapeDtypeStruct((2 * kept, BR, width), BF16)
        grads = call(
            functools.partial(backward_kernel, heads, spans),
            (span_shape,) * RING + (kv_shape,) + (back_shape,) * (RING - 1),
            [SMEM] + [ANY] * 16,
            (ANY,) * (2 * RING),
            [
                pltpu.VMEM(twin_rows, BF16),
                pltpu.VMEM(twin_rows, BF16),
                pltpu.VMEM((RING, 2 * per_ring, BR, width), BF16),
                pltpu.VMEM((RING,) + stat_shape.shape, F32),
                pltpu.VMEM((RING,) + span_shape.shape, BF16),
                pltpu.VMEM((RING * spans + 1, SPAN, width), F32),
                pltpu.VMEM((per_ring + 1, BR, width), F32),
                pltpu.VMEM((per_ring + 1, BR, width), F32),
                pltpu.SMEM((2 * RING * (RING * spans * NEIGH + 1),), jnp.int32),
                pltpu.SMEM((RING,), jnp.int32),
                pltpu.SMEM((RING * per_ring,), jnp.int32),
                dma((RING, heads)),
                dma((RING, heads)),
                dma((4 * RING,)),
            ],
            (10**11, 24 * MIB),
            meta,
            *q_now,
            *g_all,
            *kv_now,
            *stats_all,
        )
        back_blocks = spread(grads[RING:], True, -1)
        back_queries = spread(grads[:RING], False, -1)
        d_queries = sum(part.astype(F32) for part in back_queries).astype(BF16)
        d_queries = d_queries.reshape(tokens, width)
        return (d_queries,) + tuple(
            call(
                unpack_kernel,
                (block_out, block_out),
                [SMEM] + [ANY] * RING,
                (ANY, ANY),
                [
                    pltpu.VMEM((2 * RING * per_ring + 1, BR, width), BF16),
                    dma((RING,)),
                    dma((2, blocks)),
                ],
                (0, 16 * MIB),
                unpack_meta,
                *back_blocks,
            )
        )

    d_queries, d_keys, d_values = backward(per_ring)
    return (
        mixed,
        d_queries,
        d_keys.reshape(blocks * BR, width),
        d_values.reshape(blocks * BR, width),
    )


def solution(mesh):
    placed = (
        P("seq", "tp"),
        P("seq", "tp"),
        P("seq", "tp"),
        P("tp", None),
        P(("seq", "tp"), None),
        P("seq", None),
        P("seq"),
        P("seq"),
    )
    return jax.shard_map(
        on_device,
        mesh=mesh,
        in_specs=placed,
        out_specs=(P(("seq", "tp"), None), P("seq", "tp"), P("seq", "tp"), P("seq", "tp")),
        check_vma=False,
    )
```

```python
import functools

import jax
import jax.numpy as jnp
from jax import lax
from jax.experimental import pallas as pl
from jax.experimental.pallas import tpu as pltpu
from jax.sharding import PartitionSpec as P

HD = 128
SPAN = 64
BR = 128
NEIGH = 2
CAP = 2
RING = 4
DEAD = 16.0
DEAD_EDGE = 12.0
NEG = -1e30
F32 = jnp.float32
BF16 = jnp.bfloat16
SMEM = pl.BlockSpec(memory_space=pltpu.SMEM)
VMEM = pl.BlockSpec(memory_space=pltpu.VMEM)
ANY = pl.BlockSpec(memory_space=pl.ANY)
NT = (((1,), (1,)), ((), ()))
NN = (((1,), (0,)), ((), ()))
TN = (((0,), (0,)), ((), ()))
MIB = 1 << 20
PLACE = 3


def dot(a, b, dims):
    return lax.dot_general(a, b, dims, preferred_element_type=F32)


def split_seq(meta, index):
    high, low = index // RING, index % RING
    first = meta[0] == 0
    return jnp.where(first, high, low), jnp.where(first, low, high)


def block_places(meta, blocks):
    dest = [meta[PLACE + j] for j in range(blocks)]
    places = []
    for j in range(blocks):
        rank = jnp.int32(0)
        for i in range(j):
            rank = rank + jnp.where(dest[i] == dest[j], 1, 0)
        to_a, to_b = split_seq(meta, dest[j])
        places.append(((to_a - meta[1] + RING) % RING, to_b * CAP + rank))
    return places


def pack_kernel(meta, keys, values, p0, p1, p2, p3, held, in_sem, out_sem):
    packed = (p0, p1, p2, p3)
    blocks = held.shape[1]
    per_ring = RING * CAP
    reads = [
        [pltpu.make_async_copy(src.at[j], held.at[t, j], in_sem.at[t, j]) for j in range(blocks)]
        for t, src in enumerate((keys, values))
    ]
    for j in range(blocks):
        reads[0][j].start()
        reads[1][j].start()
    places = block_places(meta, blocks)
    row = lax.broadcasted_iota(jnp.int32, (BR, HD), 0)
    for j, (shift, pos) in enumerate(places):
        reads[0][j].wait()
        first = held[0, j, :, :HD].astype(F32)
        valid = meta[PLACE + blocks + j]
        held[0, j, :, :HD] = jnp.where(row < valid, first, DEAD).astype(BF16)
        reads[1][j].wait()
        for d in range(RING):

            @pl.when(shift == d)
            def _():
                for t in range(2):
                    to = packed[d].at[pos + t * per_ring]
                    pltpu.make_async_copy(held.at[t, j], to, out_sem.at[t, j]).start()

    for j in range(blocks):
        for t in range(2):
            pltpu.make_async_copy(held.at[t, j], packed[0].at[0], out_sem.at[t, j]).wait()


def unpack_kernel(meta, p0, p1, p2, p3, d_keys, d_values, held, in_sem, out_sem):
    packed = (p0, p1, p2, p3)
    outs = (d_keys, d_values)
    blocks = d_keys.shape[0]
    per_ring = RING * CAP
    reads = [pltpu.make_async_copy(packed[d], held.at[d], in_sem.at[d]) for d in range(RING)]
    for read in reads:
        read.start()
    writes = []
    places = block_places(meta, blocks)
    for read in reads:
        read.wait()
    for j, (shift, pos) in enumerate(places):
        for t in range(2):
            src = held.at[shift, pos + t * per_ring]
            writes.append(pltpu.make_async_copy(src, outs[t].at[j], out_sem.at[t, j]))
            writes[-1].start()
    for write in writes:
        write.wait()


def locate(meta, spans, i, n):
    d = i // spans
    slot = meta[PLACE + i * NEIGH + n]
    from_a, from_b = split_seq(meta, slot // CAP)
    to_b = (meta[2] - d + RING) % RING
    block = (meta[1] - from_a + RING) % RING * (RING * CAP) + to_b * CAP + slot % CAP
    return block, from_b == meta[2]


def diagonal_reads(src, buf, d, spans, heads, sem):
    reads = []
    for h in range(heads):
        at = h % 2
        to = buf.at[
            pl.ds(d * spans, spans), h // 2, pl.ds(at * SPAN, SPAN), pl.ds(at * HD, HD)
        ]
        here = src.at[pl.ds(0, spans), :, pl.ds(h * HD, HD)]
        reads.append(pltpu.make_async_copy(here, to, sem.at[h]))
    return reads


def clear_others(buf):
    count = buf.shape[0]

    def one(i, _):
        for t in range(buf.shape[1]):
            buf[i, t, :SPAN, HD:] = jnp.zeros((SPAN, HD), BF16)
            buf[i, t, SPAN:, :HD] = jnp.zeros((SPAN, HD), BF16)
        return 0

    lax.fori_loop(0, count, one, 0)


def forward_kernel(heads, spans, *args):
    meta, queries, blocks_in, outs = args[0], args[1:5], args[5:9], args[9:13]
    q_buf, kv_buf, o_buf, s_buf, spans_at, counts, q_sem, sem = args[13:]
    tokens = spans * SPAN
    per_ring = RING * CAP
    twins = heads // 2
    reads = []
    for d in range(RING):
        reads += diagonal_reads(queries[d], q_buf, d, spans, heads, q_sem.at[d])
    block_reads = [
        pltpu.make_async_copy(blocks_in[d], kv_buf.at[d], sem.at[RING + d]) for d in range(RING)
    ]
    for copy in reads + block_reads:
        copy.start()
    for r in range(RING + 1):
        counts[r] = 0
    stride = 3 * (RING * spans + 1)

    def listed(i, _):
        block0, here0 = locate(meta, spans, i, 0)
        block1, here1 = locate(meta, spans, i, 1)
        first = jnp.where(here0, block0, block1)
        which = jnp.where(jnp.logical_and(here0, here1), RING, first // per_ring)
        at = which * stride + 3 * counts[which]
        spans_at[at] = i
        spans_at[at + 1] = first
        spans_at[at + 2] = block1
        counts[which] = counts[which] + jnp.where(jnp.logical_or(here0, here1), 1, 0)
        return 0

    lax.fori_loop(0, RING * spans, listed, 0)
    clear_others(q_buf)
    o_buf[:, :tokens, :] = jnp.zeros((RING, tokens, heads * HD), BF16)
    s_buf[...] = jnp.full(s_buf.shape, NEG, F32)
    for copy in reads:
        copy.wait()
    scale = HD ** (-0.5)

    def span(i, at):
        d, g = i // spans, i % spans
        rows = pl.ds(pl.multiple_of(g * SPAN, SPAN), SPAN)
        where = [(b // per_ring, b % per_ring) for b in at]
        live = [kv_buf[r, p, :, :HD][:, :1].astype(F32) < DEAD_EDGE for r, p in where]
        for t in range(twins):
            cols = slice(2 * t * HD, 2 * (t + 1) * HD)
            q = q_buf[i, t]
            scores = [
                jnp.where(here, dot(kv_buf[r, p, :, cols], q, NT) * scale, NEG)
                for here, (r, p) in zip(live, where)
            ]
            top = functools.reduce(jnp.maximum, [jnp.max(s, axis=0, keepdims=True) for s in scores])
            terms = [jnp.exp(s - top) for s in scores]
            total = sum(jnp.sum(e, axis=0, keepdims=True) for e in terms)
            share = 1.0 / total
            mixed = sum(
                dot((e * share).astype(BF16), kv_buf[r, per_ring + p, :, cols], TN)
                for e, (r, p) in zip(terms, where)
            ).astype(BF16)
            o_buf[d, rows, 2 * t * HD : (2 * t + 1) * HD] = mixed[:SPAN, :HD]
            o_buf[d, rows, (2 * t + 1) * HD : 2 * (t + 1) * HD] = mixed[SPAN:, HD:]
            s_buf[pl.ds(i * twins + t, 1), :] = top + jnp.log(total)

    for r in range(RING + 1):
        count = counts[r]

        def two(t, _):
            for u in range(2):
                at = r * stride + 3 * jnp.minimum(2 * t + u, count - 1)
                span(spans_at[at], [spans_at[at + 1 + n] for n in range(2 if r == RING else 1)])
            return 0

        if r < RING:
            block_reads[r].wait()
        lax.fori_loop(0, (count + 1) // 2, two, 0)

    out_copies = []
    rows_in = spans * twins
    for d in range(RING):
        part = s_buf[d * rows_in : (d + 1) * rows_in, :]
        for t in range(3):
            piece = part.astype(BF16)
            o_buf[d, tokens:, t * HD : (t + 1) * HD] = piece
            part = part - piece.astype(F32)
        out_copies.append(pltpu.make_async_copy(o_buf.at[d], outs[d], sem.at[d]))
        out_copies[-1].start()
    for copy in out_copies:
        copy.wait()


def merge_kernel(heads, *args):
    parts, d_att = args[0:4], args[4]
    out, stats_out, lse_buf = args[5:]
    tokens = out.shape[0]
    spans = tokens // SPAN
    twins = heads // 2
    stat_rows = spans * twins
    for d in range(RING):
        pieces = [parts[d][tokens:, t * HD : (t + 1) * HD].astype(F32) for t in range(3)]
        lse_buf[d] = pieces[0] + pieces[1] + pieces[2]
    top = functools.reduce(jnp.maximum, [lse_buf[d] for d in range(RING)])
    total = sum(jnp.exp(lse_buf[d] - top) for d in range(RING))
    whole = top + jnp.log(total)
    stats_out[:stat_rows, :] = whole
    for d in range(RING):
        lse_buf[d] = jnp.exp(lse_buf[d] - whole)
    token = lax.broadcasted_iota(jnp.int32, (SPAN, HD), 0)
    lane = lax.broadcasted_iota(jnp.int32, (SPAN, HD), 1)
    diagonal = (token == lane, token + SPAN == lane)

    def span(g, _):
        rows = pl.ds(pl.multiple_of(g * SPAN, SPAN), SPAN)
        for t in range(twins):
            row_dots = []
            for u in range(2):
                h = 2 * t + u
                cols = slice(h * HD, (h + 1) * HD)
                acc = jnp.zeros((SPAN, HD), F32)
                for d in range(RING):
                    row = lse_buf[d, pl.ds(g * twins + t, 1), :]
                    weight = jnp.sum(jnp.where(diagonal[u], row, 0.0), axis=1, keepdims=True)
                    acc += weight * parts[d][rows, cols].astype(F32)
                out[rows, cols] = acc.astype(BF16)
                row_dot = jnp.sum(acc * d_att[rows, cols].astype(F32), axis=1, keepdims=True)
                row_dots.append(jnp.where(diagonal[u], row_dot, 0.0))
            stats_out[pl.ds(stat_rows + g * twins + t, 1), :] = jnp.sum(
                row_dots[0] + row_dots[1], axis=0, keepdims=True
            )
        return 0

    lax.fori_loop(0, spans, span, 0)


def backward_kernel(heads, spans, last, *args):
    meta, queries, d_atts, blocks_in, stats = args[0], args[1:5], args[5:9], args[9:13], args[13:17]
    if last:
        rings = loaded = (0,)
        d_blocks, args = {0: args[17]}, args[18:]
    else:
        rings, loaded = (1, 3, 2), (1, 3, 2, 0)
        d_blocks, d_qs, args = {r: args[16 + r] for r in rings}, args[20:24], args[24:]
        dq_buf, dq_acc = args[-2:]
    q_buf, g_buf, kv_buf, s_buf, dk_acc, dv_acc, pairs, counts, seen, q_sem, g_sem, sem = args[:12]
    per_ring = RING * CAP
    twins = heads // 2
    stat_rows = spans * twins
    reads = []
    for d in range(RING):
        reads += diagonal_reads(queries[d], q_buf, d, spans, heads, q_sem.at[d])
        reads += diagonal_reads(d_atts[d], g_buf, d, spans, heads, g_sem.at[d])
        reads.append(pltpu.make_async_copy(stats[d], s_buf.at[d], sem.at[4 * d]))
    block_reads = {
        r: pltpu.make_async_copy(blocks_in[r], kv_buf.at[r], sem.at[4 * r + 3]) for r in loaded
    }
    for copy in reads:
        copy.start()
    for r in loaded:
        block_reads[r].start()
    for r in range(RING):
        counts[r] = 0
    for b in range(RING * per_ring):
        seen[b] = 0
    stride = 2 * (RING * spans * NEIGH + 1)

    def listed(i, _):
        for n in range(NEIGH):
            block, here = locate(meta, spans, i, n)
            which = block // per_ring
            at = which * stride + 2 * counts[which]
            pairs[at] = i
            pairs[at + 1] = block % per_ring
            counts[which] = counts[which] + jnp.where(here, 1, 0)
            seen[block] = jnp.where(here, 1, seen[block])
        return 0

    lax.fori_loop(0, RING * spans, listed, 0)
    clear_others(q_buf)
    clear_others(g_buf)
    if not last:
        dq_acc[...] = jnp.zeros(dq_acc.shape, F32)
    for copy in reads:
        copy.wait()
    scale = HD ** (-0.5)
    writes = []
    for r in loaded:
        count = counts[r]

        def clear(p, _):
            @pl.when(seen[r * per_ring + p] == 1)
            def _():
                dk_acc[p] = jnp.zeros((BR, heads * HD), F32)
                dv_acc[p] = jnp.zeros((BR, heads * HD), F32)

            return 0

        def two(t, _):
            found = []
            for u in range(2):
                at = r * stride + 2 * jnp.minimum(2 * t + u, count - 1)
                i, p = pairs[at], pairs[at + 1]
                d, g = i // spans, i % spans
                live = kv_buf[r, p, :, :HD][:, :1].astype(F32) < DEAD_EDGE
                real = 2 * t + u < count
                to = (jnp.where(real, i, RING * spans), jnp.where(real, p, per_ring))
                for w in range(twins):
                    cols = slice(2 * w * HD, 2 * (w + 1) * HD)
                    q, g_att = q_buf[i, w], g_buf[i, w]
                    k = kv_buf[r, p, :, cols]
                    v = kv_buf[r, per_ring + p, :, cols]
                    lse = s_buf[d, pl.ds(g * twins + w, 1), :]
                    row_dot = s_buf[d, pl.ds(stat_rows + g * twins + w, 1), :]
                    prob = jnp.where(live, jnp.exp(dot(k, q, NT) * scale - lse), 0.0)
                    d_s = (prob * (dot(v, g_att, NT) - row_dot)).astype(BF16)
                    gives = [None, None, None]
                    if r in rings:
                        gives[:2] = dot(prob.astype(BF16), g_att, NN), dot(d_s, q, NN)
                    if not last:
                        gives[2] = dot(d_s, k, TN)
                    found.append((to, w, *gives))
            for (i, p), w, d_v, d_k, d_q in found:
                cols = slice(2 * w * HD, 2 * (w + 1) * HD)
                if r in rings:
                    dv_acc[p, :, cols] += d_v
                    dk_acc[p, :, cols] += d_k
                if not last:
                    dq_acc[i, :, 2 * w * HD : (2 * w + 1) * HD] += d_q[:SPAN, :HD]
                    dq_acc[i, :, (2 * w + 1) * HD : 2 * (w + 1) * HD] += d_q[SPAN:, HD:]
            return 0

        def finish(p, _):
            one = seen[r * per_ring + p]

            @pl.when(one == 1)
            def _():
                kv_buf[r, p] = (dk_acc[p] * scale).astype(BF16)
                kv_buf[r, per_ring + p] = dv_acc[p].astype(BF16)

            @pl.when(one == 0)
            def _():
                kv_buf[r, p] = jnp.zeros((BR, heads * HD), BF16)
                kv_buf[r, per_ring + p] = jnp.zeros((BR, heads * HD), BF16)

            return 0

        if r in rings:
            lax.fori_loop(0, per_ring, clear, 0)
        block_reads[r].wait()
        lax.fori_loop(0, (count + 1) // 2, two, 0)
        if r in rings:
            lax.fori_loop(0, per_ring, finish, 0)
            writes.append(pltpu.make_async_copy(kv_buf.at[r], d_blocks[r], sem.at[4 * r + 3]))
            writes[-1].start()
    if not last:
        for d in range(RING):
            for g in range(spans):
                dq_buf[d, g] = (dq_acc[d * spans + g] * scale).astype(BF16)
            writes.append(pltpu.make_async_copy(dq_buf.at[d], d_qs[d], sem.at[4 * d + 1]))
            writes[-1].start()
    for write in writes:
        write.wait()


def call(kernel, outs, in_specs, out_specs, scratch, cost, *operands, vmem=58):
    return pl.pallas_call(
        kernel,
        out_shape=outs,
        in_specs=in_specs,
        out_specs=out_specs,
        scratch_shapes=scratch,
        compiler_params=pltpu.CompilerParams(vmem_limit_bytes=vmem * MIB),
        cost_estimate=pl.CostEstimate(flops=cost[0], bytes_accessed=cost[1], transcendentals=0),
    )(*operands)


def on_device(
    queries, nb_keys, nb_values, out_weight, out_grad, span_refs, block_dest, block_valid
):
    seq_count = lax.axis_size("seq")
    tp_count = lax.axis_size("tp")
    tokens, width = queries.shape
    heads = width // HD
    spans = tokens // SPAN
    blocks = block_dest.shape[0]
    per_ring = RING * CAP
    stat_rows = spans * heads // 2
    ref_count = spans * NEIGH
    dma = pltpu.SemaphoreType.DMA

    seq_at = lax.axis_index("seq")
    core = lax.axis_index("tp") % 2
    high, low = seq_at // RING, seq_at % RING
    place = jnp.stack(
        [core, jnp.where(core == 0, high, low), jnp.where(core == 0, low, high)]
    ).astype(jnp.int32)

    def ring_pairs(shift, along_a):
        pairs = []
        for s in range(seq_count):
            z, y = s // RING, s % RING
            for t in range(tp_count):
                if (t % 2 == 0) == along_a:
                    to = (z + shift) % RING * RING + y
                else:
                    to = z * RING + (y + shift) % RING
                pairs.append((s * tp_count + t, to * tp_count + t))
        return pairs

    def move(x, shift, along_a):
        return lax.ppermute(x, ("seq", "tp"), ring_pairs(shift % RING, along_a))

    order = (1, 3, 2)

    def spread(parts, along_a, sign):
        got = {0: parts[0]}
        for d in order:
            got[d] = move(parts[d], sign * d, along_a)
        return tuple(got[d] for d in range(RING))

    grad_rows = lax.all_gather(out_grad, "tp", axis=0, tiled=True)

    slot_count = seq_count * CAP
    ref_rows = jnp.pad(
        span_refs.astype(BF16).reshape(1, 1, ref_count),
        ((0, 0), (0, SPAN - 1), (0, width - ref_count)),
    )
    q_sent = jnp.concatenate([queries.reshape(spans, SPAN, width), ref_rows], axis=0)
    q_all = spread((q_sent,) * RING, False, 1)
    refs = jnp.concatenate([q[spans, 0, :ref_count] for q in q_all]).astype(jnp.int32)
    meta = jnp.concatenate([place, refs])
    pack_meta = jnp.concatenate([place, block_dest, block_valid])

    kv_shape = jax.ShapeDtypeStruct((2 * per_ring, BR, width), BF16)
    packed = call(
        pack_kernel,
        (kv_shape,) * RING,
        [SMEM, ANY, ANY],
        (ANY,) * RING,
        [
            pltpu.VMEM((2, blocks, BR, width), BF16),
            dma((2, blocks)),
            dma((2, blocks)),
        ],
        (0, 16 * MIB),
        pack_meta,
        nb_keys.reshape(blocks, BR, width),
        nb_values.reshape(blocks, BR, width),
    )
    kv_all = spread(packed, True, 1)

    d_attended = lax.dot_general(
        grad_rows, out_weight, (((1,), (1,)), ((), ())), preferred_element_type=F32
    ).astype(BF16)
    g_all = spread((d_attended.reshape(spans, SPAN, width),) * RING, False, 1)

    kv_now, q_now, d_attended = lax.optimization_barrier((kv_all, q_all, d_attended))
    twin_rows = (RING * spans, heads // 2, 2 * SPAN, 2 * HD)
    part_shape = jax.ShapeDtypeStruct((tokens + stat_rows, width), BF16)
    found = call(
        functools.partial(forward_kernel, heads, spans),
        (part_shape,) * RING,
        [SMEM] + [ANY] * 8,
        (ANY,) * RING,
        [
            pltpu.VMEM(twin_rows, BF16),
            pltpu.VMEM((RING, 2 * per_ring, BR, width), BF16),
            pltpu.VMEM((RING, tokens + stat_rows, width), BF16),
            pltpu.VMEM((RING * stat_rows, HD), F32),
            pltpu.SMEM((3 * (RING + 1) * (RING * spans + 1),), jnp.int32),
            pltpu.SMEM((RING + 1,), jnp.int32),
            dma((RING, heads)),
            dma((2 * RING,)),
        ],
        (10**11, 12 * MIB),
        meta,
        *q_now,
        *kv_now,
    )
    parts = spread(found, False, -1)
    span_shape = jax.ShapeDtypeStruct((spans, SPAN, width), BF16)
    rows_shape = jax.ShapeDtypeStruct((tokens, width), BF16)
    stat_shape = jax.ShapeDtypeStruct((2 * stat_rows, HD), F32)
    attended, stats = call(
        functools.partial(merge_kernel, heads),
        (rows_shape, stat_shape),
        [VMEM] * 5,
        (VMEM, VMEM),
        [pltpu.VMEM((RING, stat_rows, HD), F32)],
        (10**11, 4 * MIB),
        *parts,
        d_attended,
        vmem=40,
    )
    stats_all = spread((stats,) * RING, False, 1)
    attended, g_all = lax.optimization_barrier((attended, g_all))
    partial = jnp.dot(attended, out_weight, preferred_element_type=F32).astype(BF16)
    mixed = lax.psum_scatter(partial, "tp", scatter_dimension=0, tiled=True)

    block_out = jax.ShapeDtypeStruct((blocks, BR, width), BF16)

    def backward(last, queries_in, sent_in, stats_in):
        scratch = [
            pltpu.VMEM(twin_rows, BF16),
            pltpu.VMEM(twin_rows, BF16),
            pltpu.VMEM((RING, 2 * per_ring, BR, width), BF16),
            pltpu.VMEM((RING,) + stat_shape.shape, F32),
            pltpu.VMEM((per_ring + 1, BR, width), F32),
            pltpu.VMEM((per_ring + 1, BR, width), F32),
            pltpu.SMEM((2 * RING * (RING * spans * NEIGH + 1),), jnp.int32),
            pltpu.SMEM((RING,), jnp.int32),
            pltpu.SMEM((RING * per_ring,), jnp.int32),
            dma((RING, heads)),
            dma((RING, heads)),
            dma((4 * RING,)),
        ]
        outs = (kv_shape,)
        if not last:
            outs = (kv_shape,) * (RING - 1) + (span_shape,) * RING
            scratch.append(pltpu.VMEM((RING,) + span_shape.shape, BF16))
            scratch.append(pltpu.VMEM((RING * spans + 1, SPAN, width), F32))
        return call(
            functools.partial(backward_kernel, heads, spans, last),
            outs,
            [SMEM] + [ANY] * 16,
            (ANY,) * len(outs),
            scratch,
            (10**11, 24 * MIB),
            meta,
            *queries_in,
            *sent_in,
            *kv_now,
            *stats_in,
        )

    grads = backward(False, q_now, g_all, stats_all)
    back_blocks = spread((None,) + grads[: RING - 1], True, -1)[1:]
    back_queries = spread(grads[RING - 1 :], False, -1)
    q_late, _ = lax.optimization_barrier((q_now, grads[0]))
    (own_blocks,) = backward(True, q_late, g_all, stats_all)
    d_queries = sum(part.astype(F32) for part in back_queries).astype(BF16)
    d_queries = d_queries.reshape(tokens, width)
    d_keys, d_values = call(
        unpack_kernel,
        (block_out, block_out),
        [SMEM] + [ANY] * RING,
        (ANY, ANY),
        [
            pltpu.VMEM((RING, 2 * per_ring, BR, width), BF16),
            dma((RING,)),
            dma((2, blocks)),
        ],
        (0, 16 * MIB),
        pack_meta,
        own_blocks,
        *back_blocks,
    )
    return (
        mixed,
        d_queries,
        d_keys.reshape(blocks * BR, width),
        d_values.reshape(blocks * BR, width),
    )


def solution(mesh):
    placed = (
        P("seq", "tp"),
        P("seq", "tp"),
        P("seq", "tp"),
        P("tp", None),
        P(("seq", "tp"), None),
        P("seq", None),
        P("seq"),
        P("seq"),
    )
    return jax.shard_map(
        on_device,
        mesh=mesh,
        in_specs=placed,
        out_specs=(P(("seq", "tp"), None), P("seq", "tp"), P("seq", "tp"), P("seq", "tp")),
        check_vma=False,
    )
```

```python
import functools

import jax
import jax.numpy as jnp
from jax import lax
from jax.experimental import pallas as pl
from jax.experimental.pallas import tpu as pltpu
from jax.sharding import PartitionSpec as P

HD = 128
SPAN = 64
BR = 128
NEIGH = 2
CAP = 2
RING = 4
DEAD = 16.0
DEAD_EDGE = 12.0
NEG = -1e30
F32 = jnp.float32
BF16 = jnp.bfloat16
SMEM = pl.BlockSpec(memory_space=pltpu.SMEM)
VMEM = pl.BlockSpec(memory_space=pltpu.VMEM)
ANY = pl.BlockSpec(memory_space=pl.ANY)
NT = (((1,), (1,)), ((), ()))
NN = (((1,), (0,)), ((), ()))
TN = (((0,), (0,)), ((), ()))
MIB = 1 << 20
PLACE = 3
ELSEWHERE = RING * RING * CAP


def dot(a, b, dims):
    return lax.dot_general(a, b, dims, preferred_element_type=F32)


def split_seq(meta, index):
    high, low = index // RING, index % RING
    first = meta[0] == 0
    return jnp.where(first, high, low), jnp.where(first, low, high)


def block_places(meta, blocks):
    dest = [meta[PLACE + j] for j in range(blocks)]
    places = []
    for j in range(blocks):
        rank = jnp.int32(0)
        for i in range(j):
            rank = rank + jnp.where(dest[i] == dest[j], 1, 0)
        to_a, to_b = split_seq(meta, dest[j])
        places.append(((to_a - meta[1] + RING) % RING, to_b * CAP + rank))
    return places


def pack_kernel(meta, keys, values, p0, p1, p2, p3, held, in_sem, out_sem):
    packed = (p0, p1, p2, p3)
    blocks = held.shape[1]
    per_ring = RING * CAP
    reads = [
        [pltpu.make_async_copy(src.at[j], held.at[t, j], in_sem.at[t, j]) for j in range(blocks)]
        for t, src in enumerate((keys, values))
    ]
    for j in range(blocks):
        reads[0][j].start()
        reads[1][j].start()
    places = block_places(meta, blocks)
    row = lax.broadcasted_iota(jnp.int32, (BR, HD), 0)
    for j, (shift, pos) in enumerate(places):
        reads[0][j].wait()
        first = held[0, j, :, :HD].astype(F32)
        valid = meta[PLACE + blocks + j]
        held[0, j, :, :HD] = jnp.where(row < valid, first, DEAD).astype(BF16)
        reads[1][j].wait()
        for d in range(RING):

            @pl.when(shift == d)
            def _():
                for t in range(2):
                    to = packed[d].at[pos + t * per_ring]
                    pltpu.make_async_copy(held.at[t, j], to, out_sem.at[t, j]).start()

    for j in range(blocks):
        for t in range(2):
            pltpu.make_async_copy(held.at[t, j], packed[0].at[0], out_sem.at[t, j]).wait()


def unpack_kernel(meta, p0, p1, p2, p3, d_keys, d_values, held, in_sem, out_sem):
    packed = (p0, p1, p2, p3)
    outs = (d_keys, d_values)
    blocks = d_keys.shape[0]
    per_ring = RING * CAP
    for d in range(RING):

        def one(p, _):
            j = meta[d * per_ring + p]

            @pl.when(j < blocks)
            def _():
                for t in range(2):
                    src = packed[d].at[p + t * per_ring]
                    pltpu.make_async_copy(src, held.at[t, j], in_sem.at[t, j]).start()

            return 0

        lax.fori_loop(0, per_ring, one, 0)
    writes = []
    for t in range(2):
        for j in range(blocks):
            pltpu.make_async_copy(packed[0].at[0], held.at[t, j], in_sem.at[t, j]).wait()
        writes.append(pltpu.make_async_copy(held.at[t], outs[t], out_sem.at[t]))
        writes[-1].start()
    for write in writes:
        write.wait()


def locate(meta, i, n):
    at = meta[PLACE + i * NEIGH + n]
    return at % ELSEWHERE, at < ELSEWHERE


def diagonal_reads(src, buf, d, spans, heads, sem):
    reads = []
    for h in range(heads):
        at = h % 2
        to = buf.at[
            pl.ds(d * spans, spans), h // 2, pl.ds(at * SPAN, SPAN), pl.ds(at * HD, HD)
        ]
        here = src.at[pl.ds(0, spans), :, pl.ds(h * HD, HD)]
        reads.append(pltpu.make_async_copy(here, to, sem.at[h]))
    return reads


def clear_others(buf):
    count = buf.shape[0]

    def one(i, _):
        for t in range(buf.shape[1]):
            buf[i, t, :SPAN, HD:] = jnp.zeros((SPAN, HD), BF16)
            buf[i, t, SPAN:, :HD] = jnp.zeros((SPAN, HD), BF16)
        return 0

    lax.fori_loop(0, count, one, 0)


def forward_kernel(heads, spans, *args):
    meta, queries, blocks_in, outs = args[0], args[1:5], args[5:9], args[9:13]
    q_buf, kv_buf, o_buf, s_buf, spans_at, counts, q_sem, sem = args[13:]
    tokens = spans * SPAN
    per_ring = RING * CAP
    twins = heads // 2
    reads = []
    for d in range(RING):
        reads += diagonal_reads(queries[d], q_buf, d, spans, heads, q_sem.at[d])
    block_reads = [
        pltpu.make_async_copy(blocks_in[d], kv_buf.at[d], sem.at[RING + d]) for d in range(RING)
    ]
    for copy in reads + block_reads:
        copy.start()
    for r in range(RING + 1):
        counts[r] = 0
    stride = 3 * (RING * spans + 1)

    def listed(i, _):
        block0, here0 = locate(meta, i, 0)
        block1, here1 = locate(meta, i, 1)
        first = jnp.where(here0, block0, block1)
        which = jnp.where(jnp.logical_and(here0, here1), RING, first // per_ring)
        at = which * stride + 3 * counts[which]
        spans_at[at] = i
        spans_at[at + 1] = first
        spans_at[at + 2] = block1
        counts[which] = counts[which] + jnp.where(jnp.logical_or(here0, here1), 1, 0)
        return 0

    lax.fori_loop(0, RING * spans, listed, 0)
    clear_others(q_buf)
    o_buf[:, :tokens, :] = jnp.zeros((RING, tokens, heads * HD), BF16)
    s_buf[...] = jnp.full(s_buf.shape, NEG, F32)
    for copy in reads:
        copy.wait()
    scale = HD ** (-0.5)

    def span(i, at):
        d, g = i // spans, i % spans
        rows = pl.ds(pl.multiple_of(g * SPAN, SPAN), SPAN)
        where = [(b // per_ring, b % per_ring) for b in at]
        live = [kv_buf[r, p, :, :HD][:, :1].astype(F32) < DEAD_EDGE for r, p in where]
        for t in range(twins):
            cols = slice(2 * t * HD, 2 * (t + 1) * HD)
            q = q_buf[i, t]
            scores = [
                jnp.where(here, dot(kv_buf[r, p, :, cols], q, NT) * scale, NEG)
                for here, (r, p) in zip(live, where)
            ]
            top = functools.reduce(jnp.maximum, [jnp.max(s, axis=0, keepdims=True) for s in scores])
            terms = [jnp.exp(s - top) for s in scores]
            total = sum(jnp.sum(e, axis=0, keepdims=True) for e in terms)
            share = 1.0 / total
            mixed = sum(
                dot((e * share).astype(BF16), kv_buf[r, per_ring + p, :, cols], TN)
                for e, (r, p) in zip(terms, where)
            ).astype(BF16)
            o_buf[d, rows, 2 * t * HD : (2 * t + 1) * HD] = mixed[:SPAN, :HD]
            o_buf[d, rows, (2 * t + 1) * HD : 2 * (t + 1) * HD] = mixed[SPAN:, HD:]
            s_buf[pl.ds(i * twins + t, 1), :] = top + jnp.log(total)

    for r in range(RING + 1):
        count = counts[r]

        def two(t, _):
            for u in range(2):
                at = r * stride + 3 * jnp.minimum(2 * t + u, count - 1)
                span(spans_at[at], [spans_at[at + 1 + n] for n in range(2 if r == RING else 1)])
            return 0

        if r < RING:
            block_reads[r].wait()
        lax.fori_loop(0, (count + 1) // 2, two, 0)

    out_copies = []
    rows_in = spans * twins
    for d in range(RING):
        part = s_buf[d * rows_in : (d + 1) * rows_in, :]
        for t in range(3):
            piece = part.astype(BF16)
            o_buf[d, tokens:, t * HD : (t + 1) * HD] = piece
            part = part - piece.astype(F32)
        out_copies.append(pltpu.make_async_copy(o_buf.at[d], outs[d], sem.at[d]))
        out_copies[-1].start()
    for copy in out_copies:
        copy.wait()


def merge_kernel(heads, *args):
    parts, d_att = args[0:4], args[4]
    out, stats_out, lse_buf = args[5:]
    tokens = out.shape[0]
    spans = tokens // SPAN
    twins = heads // 2
    stat_rows = spans * twins
    for d in range(RING):
        pieces = [parts[d][tokens:, t * HD : (t + 1) * HD].astype(F32) for t in range(3)]
        lse_buf[d] = pieces[0] + pieces[1] + pieces[2]
    top = functools.reduce(jnp.maximum, [lse_buf[d] for d in range(RING)])
    total = sum(jnp.exp(lse_buf[d] - top) for d in range(RING))
    whole = top + jnp.log(total)
    stats_out[:stat_rows, :] = whole
    for d in range(RING):
        lse_buf[d] = jnp.exp(lse_buf[d] - whole)
    token = lax.broadcasted_iota(jnp.int32, (SPAN, HD), 0)
    lane = lax.broadcasted_iota(jnp.int32, (SPAN, HD), 1)
    diagonal = (token == lane, token + SPAN == lane)

    def span(g, _):
        rows = pl.ds(pl.multiple_of(g * SPAN, SPAN), SPAN)
        for t in range(twins):
            row_dots = []
            for u in range(2):
                h = 2 * t + u
                cols = slice(h * HD, (h + 1) * HD)
                acc = jnp.zeros((SPAN, HD), F32)
                for d in range(RING):
                    row = lse_buf[d, pl.ds(g * twins + t, 1), :]
                    weight = jnp.sum(jnp.where(diagonal[u], row, 0.0), axis=1, keepdims=True)
                    acc += weight * parts[d][rows, cols].astype(F32)
                out[rows, cols] = acc.astype(BF16)
                row_dot = jnp.sum(acc * d_att[rows, cols].astype(F32), axis=1, keepdims=True)
                row_dots.append(jnp.where(diagonal[u], row_dot, 0.0))
            stats_out[pl.ds(stat_rows + g * twins + t, 1), :] = jnp.sum(
                row_dots[0] + row_dots[1], axis=0, keepdims=True
            )
        return 0

    lax.fori_loop(0, spans, span, 0)


def backward_kernel(heads, spans, last, *args):
    meta, queries, d_atts, blocks_in, stats = args[0], args[1:5], args[5:9], args[9:13], args[13:17]
    if last:
        rings = loaded = (0,)
        d_blocks, args = {0: args[17]}, args[18:]
    else:
        rings, loaded = (1, 3, 2), (1, 3, 2, 0)
        d_blocks, d_qs, args = {r: args[16 + r] for r in rings}, args[20:23], args[23:]
        dq_buf, dq_acc = args[-2:]
    q_buf, g_buf, kv_buf, s_buf, dk_acc, dv_acc, pairs, counts, seen, q_sem, g_sem, sem = args[:12]
    per_ring = RING * CAP
    twins = heads // 2
    stat_rows = spans * twins
    reads = []
    for d in range(RING):
        reads += diagonal_reads(queries[d], q_buf, d, spans, heads, q_sem.at[d])
        reads += diagonal_reads(d_atts[d], g_buf, d, spans, heads, g_sem.at[d])
        reads.append(pltpu.make_async_copy(stats[d], s_buf.at[d], sem.at[4 * d]))
    block_reads = {
        r: pltpu.make_async_copy(blocks_in[r], kv_buf.at[r], sem.at[4 * r + 3]) for r in loaded
    }
    for copy in reads:
        copy.start()
    for r in loaded:
        block_reads[r].start()
    for r in range(RING):
        counts[r] = 0
    for b in range(RING * per_ring):
        seen[b] = 0
    stride = 2 * (RING * spans * NEIGH + 1)

    def listed(i, _):
        for n in range(NEIGH):
            block, here = locate(meta, i, n)
            which = block // per_ring
            at = which * stride + 2 * counts[which]
            pairs[at] = i
            pairs[at + 1] = block % per_ring
            counts[which] = counts[which] + jnp.where(here, 1, 0)
            seen[block] = jnp.where(here, 1, seen[block])
        return 0

    lax.fori_loop(0, RING * spans, listed, 0)
    clear_others(q_buf)
    clear_others(g_buf)
    if not last:
        dq_acc[...] = jnp.zeros(dq_acc.shape, F32)
    for copy in reads:
        copy.wait()
    scale = HD ** (-0.5)
    writes = []
    for r in loaded:
        count = counts[r]

        def clear(p, _):
            @pl.when(seen[r * per_ring + p] == 1)
            def _():
                dk_acc[p] = jnp.zeros((BR, heads * HD), F32)
                dv_acc[p] = jnp.zeros((BR, heads * HD), F32)

            return 0

        def two(t, _):
            found = []
            for u in range(2):
                at = r * stride + 2 * jnp.minimum(2 * t + u, count - 1)
                i, p = pairs[at], pairs[at + 1]
                d, g = i // spans, i % spans
                live = kv_buf[r, p, :, :HD][:, :1].astype(F32) < DEAD_EDGE
                real = 2 * t + u < count
                to = (jnp.where(real, i, RING * spans), jnp.where(real, p, per_ring))
                for w in range(twins):
                    cols = slice(2 * w * HD, 2 * (w + 1) * HD)
                    q, g_att = q_buf[i, w], g_buf[i, w]
                    k = kv_buf[r, p, :, cols]
                    v = kv_buf[r, per_ring + p, :, cols]
                    lse = s_buf[d, pl.ds(g * twins + w, 1), :]
                    row_dot = s_buf[d, pl.ds(stat_rows + g * twins + w, 1), :]
                    prob = jnp.where(live, jnp.exp(dot(k, q, NT) * scale - lse), 0.0)
                    d_s = (prob * (dot(v, g_att, NT) - row_dot)).astype(BF16)
                    gives = [None, None, None]
                    if r in rings:
                        gives[:2] = dot(prob.astype(BF16), g_att, NN), dot(d_s, q, NN)
                    if not last:
                        gives[2] = dot(d_s, k, TN)
                    found.append((to, w, *gives))
            for (i, p), w, d_v, d_k, d_q in found:
                cols = slice(2 * w * HD, 2 * (w + 1) * HD)
                if r in rings:
                    dv_acc[p, :, cols] += d_v
                    dk_acc[p, :, cols] += d_k
                if not last:
                    dq_acc[i, :, 2 * w * HD : (2 * w + 1) * HD] += d_q[:SPAN, :HD]
                    dq_acc[i, :, (2 * w + 1) * HD : 2 * (w + 1) * HD] += d_q[SPAN:, HD:]
            return 0

        def finish(p, _):
            one = seen[r * per_ring + p]

            @pl.when(one == 1)
            def _():
                kv_buf[r, p] = (dk_acc[p] * scale).astype(BF16)
                kv_buf[r, per_ring + p] = dv_acc[p].astype(BF16)

            @pl.when(one == 0)
            def _():
                kv_buf[r, p] = jnp.zeros((BR, heads * HD), BF16)
                kv_buf[r, per_ring + p] = jnp.zeros((BR, heads * HD), BF16)

            return 0

        if r in rings:
            lax.fori_loop(0, per_ring, clear, 0)
        block_reads[r].wait()
        lax.fori_loop(0, (count + 1) // 2, two, 0)
        if r in rings:
            lax.fori_loop(0, per_ring, finish, 0)
            writes.append(pltpu.make_async_copy(kv_buf.at[r], d_blocks[r], sem.at[4 * r + 3]))
            writes[-1].start()
    if not last:
        first = jnp.where(meta[2] % 2 == 0, 3, 1)
        goes = (d_qs[0].at[0], d_qs[0].at[1], d_qs[1], d_qs[2])
        for n, (to, d) in enumerate(zip(goes, (first, RING - first, 2, 0))):
            for g in range(spans):
                dq_buf[n, g] = (dq_acc[d * spans + g] * scale).astype(BF16)
            writes.append(pltpu.make_async_copy(dq_buf.at[n], to, sem.at[4 * n + 1]))
            writes[-1].start()
    for write in writes:
        write.wait()


def call(kernel, outs, in_specs, out_specs, scratch, cost, *operands, vmem=58):
    return pl.pallas_call(
        kernel,
        out_shape=outs,
        in_specs=in_specs,
        out_specs=out_specs,
        scratch_shapes=scratch,
        compiler_params=pltpu.CompilerParams(vmem_limit_bytes=vmem * MIB),
        cost_estimate=pl.CostEstimate(flops=cost[0], bytes_accessed=cost[1], transcendentals=0),
    )(*operands)


def on_device(
    queries, nb_keys, nb_values, out_weight, out_grad, span_refs, block_dest, block_valid
):
    seq_count = lax.axis_size("seq")
    tp_count = lax.axis_size("tp")
    tokens, width = queries.shape
    heads = width // HD
    spans = tokens // SPAN
    blocks = block_dest.shape[0]
    per_ring = RING * CAP
    stat_rows = spans * heads // 2
    ref_count = spans * NEIGH
    dma = pltpu.SemaphoreType.DMA

    seq_at = lax.axis_index("seq")
    core = lax.axis_index("tp") % 2
    high, low = seq_at // RING, seq_at % RING
    place = jnp.stack(
        [core, jnp.where(core == 0, high, low), jnp.where(core == 0, low, high)]
    ).astype(jnp.int32)

    def ring_pairs(shift, along_a):
        pairs = []
        for s in range(seq_count):
            z, y = s // RING, s % RING
            for t in range(tp_count):
                if (t % 2 == 0) == along_a:
                    to = (z + shift) % RING * RING + y
                else:
                    to = z * RING + (y + shift) % RING
                pairs.append((s * tp_count + t, to * tp_count + t))
        return pairs

    def neighbour_pairs():
        pairs = []
        for s in range(seq_count):
            z, y = s // RING, s % RING
            for t in range(tp_count):
                to = z * RING + (y ^ 1) if t % 2 == 0 else (z ^ 1) * RING + y
                pairs.append((s * tp_count + t, to * tp_count + t))
        return pairs

    def move(x, shift, along_a):
        return lax.ppermute(x, ("seq", "tp"), ring_pairs(shift % RING, along_a))

    order = (1, 3, 2)

    def spread(parts, along_a, sign):
        got = {0: parts[0]}
        for d in order:
            got[d] = move(parts[d], sign * d, along_a)
        return tuple(got[d] for d in range(RING))

    grad_rows = lax.all_gather(out_grad, "tp", axis=0, tiled=True)

    slot_count = seq_count * CAP
    ref_rows = jnp.pad(
        span_refs.astype(BF16).reshape(1, 1, ref_count),
        ((0, 0), (0, SPAN - 1), (0, width - ref_count)),
    )
    q_sent = jnp.concatenate([queries.reshape(spans, SPAN, width), ref_rows], axis=0)
    q_all = spread((q_sent,) * RING, False, 1)
    refs = jnp.concatenate([q[spans, 0, :ref_count] for q in q_all]).astype(jnp.int32)
    refs = refs.reshape(RING, ref_count)
    holder = refs // CAP
    from_a = jnp.where(core == 0, holder // RING, holder % RING)
    from_b = jnp.where(core == 0, holder % RING, holder // RING)
    to_b = (place[2] - jnp.arange(RING)[:, None] + RING) % RING
    lies = (place[1] - from_a + RING) % RING * per_ring + to_b * CAP + refs % CAP
    lies = lies + jnp.where(from_b == place[2], 0, ELSEWHERE)
    meta = jnp.concatenate([place, lies.reshape(-1).astype(jnp.int32)])
    pack_meta = jnp.concatenate([place, block_dest, block_valid])

    kv_shape = jax.ShapeDtypeStruct((2 * per_ring, BR, width), BF16)
    packed = call(
        pack_kernel,
        (kv_shape,) * RING,
        [SMEM, ANY, ANY],
        (ANY,) * RING,
        [
            pltpu.VMEM((2, blocks, BR, width), BF16),
            dma((2, blocks)),
            dma((2, blocks)),
        ],
        (0, 16 * MIB),
        pack_meta,
        nb_keys.reshape(blocks, BR, width),
        nb_values.reshape(blocks, BR, width),
    )
    kv_all = spread(packed, True, 1)

    d_attended = lax.dot_general(
        grad_rows, out_weight, (((1,), (1,)), ((), ())), preferred_element_type=F32
    ).astype(BF16)
    g_all = spread((d_attended.reshape(spans, SPAN, width),) * RING, False, 1)

    kv_now, q_now, d_attended = lax.optimization_barrier((kv_all, q_all, d_attended))
    twin_rows = (RING * spans, heads // 2, 2 * SPAN, 2 * HD)
    part_shape = jax.ShapeDtypeStruct((tokens + stat_rows, width), BF16)
    found = call(
        functools.partial(forward_kernel, heads, spans),
        (part_shape,) * RING,
        [SMEM] + [ANY] * 8,
        (ANY,) * RING,
        [
            pltpu.VMEM(twin_rows, BF16),
            pltpu.VMEM((RING, 2 * per_ring, BR, width), BF16),
            pltpu.VMEM((RING, tokens + stat_rows, width), BF16),
            pltpu.VMEM((RING * stat_rows, HD), F32),
            pltpu.SMEM((3 * (RING + 1) * (RING * spans + 1),), jnp.int32),
            pltpu.SMEM((RING + 1,), jnp.int32),
            dma((RING, heads)),
            dma((2 * RING,)),
        ],
        (10**11, 12 * MIB),
        meta,
        *q_now,
        *kv_now,
    )
    parts = spread(found, False, -1)
    span_shape = jax.ShapeDtypeStruct((spans, SPAN, width), BF16)
    rows_shape = jax.ShapeDtypeStruct((tokens, width), BF16)
    stat_shape = jax.ShapeDtypeStruct((2 * stat_rows, HD), F32)
    attended, stats = call(
        functools.partial(merge_kernel, heads),
        (rows_shape, stat_shape),
        [VMEM] * 5,
        (VMEM, VMEM),
        [pltpu.VMEM((RING, stat_rows, HD), F32)],
        (10**11, 4 * MIB),
        *parts,
        d_attended,
        vmem=40,
    )
    stats_all = spread((stats,) * RING, False, 1)
    attended, g_all = lax.optimization_barrier((attended, g_all))
    partial = jnp.dot(attended, out_weight, preferred_element_type=F32).astype(BF16)
    mixed = lax.psum_scatter(partial, "tp", scatter_dimension=0, tiled=True)

    same = block_dest[:, None] == block_dest[None, :]
    lower = jnp.arange(blocks)[:, None] < jnp.arange(blocks)[None, :]
    rank = jnp.sum((same & lower).astype(jnp.int32), axis=0)
    to_a = jnp.where(core == 0, block_dest // RING, block_dest % RING)
    to_b = jnp.where(core == 0, block_dest % RING, block_dest // RING)
    came = ((to_a - place[1] + RING) % RING * per_ring + to_b * CAP + rank).astype(jnp.int32)
    hit = came[None, :] == jnp.arange(RING * per_ring)[:, None]
    came = jnp.sum(jnp.where(hit, jnp.arange(blocks)[None, :] - blocks, 0), axis=1) + blocks
    came = came.astype(jnp.int32)
    block_out = jax.ShapeDtypeStruct((blocks, BR, width), BF16)

    def backward(last, queries_in, sent_in, stats_in):
        scratch = [
            pltpu.VMEM(twin_rows, BF16),
            pltpu.VMEM(twin_rows, BF16),
            pltpu.VMEM((RING, 2 * per_ring, BR, width), BF16),
            pltpu.VMEM((RING,) + stat_shape.shape, F32),
            pltpu.VMEM((per_ring + 1, BR, width), F32),
            pltpu.VMEM((per_ring + 1, BR, width), F32),
            pltpu.SMEM((2 * RING * (RING * spans * NEIGH + 1),), jnp.int32),
            pltpu.SMEM((RING,), jnp.int32),
            pltpu.SMEM((RING * per_ring,), jnp.int32),
            dma((RING, heads)),
            dma((RING, heads)),
            dma((4 * RING,)),
        ]
        outs = (kv_shape,)
        if not last:
            away_shape = jax.ShapeDtypeStruct((2,) + span_shape.shape, BF16)
            outs = (kv_shape,) * (RING - 1) + (away_shape, span_shape, span_shape)
            scratch.append(pltpu.VMEM((RING,) + span_shape.shape, BF16))
            scratch.append(pltpu.VMEM((RING * spans + 1, SPAN, width), F32))
        return call(
            functools.partial(backward_kernel, heads, spans, last),
            outs,
            [SMEM] + [ANY] * 16,
            (ANY,) * len(outs),
            scratch,
            (10**11, 24 * MIB),
            meta,
            *queries_in,
            *sent_in,
            *kv_now,
            *stats_in,
        )

    grads = backward(False, q_now, g_all, stats_all)
    back_blocks = spread((None,) + grads[: RING - 1], True, -1)[1:]
    d_q_away, d_q_far, d_q_own = grads[RING - 1 :]
    d_q_near = lax.ppermute(d_q_away, ("seq", "tp"), neighbour_pairs())
    d_q_far = (d_q_far.astype(F32) + d_q_near[1].astype(F32)).astype(BF16)
    d_q_far = move(d_q_far, 2, False)
    q_late, _ = lax.optimization_barrier((q_now, grads[0]))
    (own_blocks,) = backward(True, q_late, g_all, stats_all)
    d_queries = sum(part.astype(F32) for part in (d_q_own, d_q_near[0], d_q_far)).astype(BF16)
    d_queries = d_queries.reshape(tokens, width)
    d_keys, d_values = call(
        unpack_kernel,
        (block_out, block_out),
        [SMEM] + [ANY] * RING,
        (ANY, ANY),
        [
            pltpu.VMEM((2, blocks, BR, width), BF16),
            dma((2, blocks)),
            dma((2,)),
        ],
        (0, 16 * MIB),
        came,
        own_blocks,
        *back_blocks,
    )
    return (
        mixed,
        d_queries,
        d_keys.reshape(blocks * BR, width),
        d_values.reshape(blocks * BR, width),
    )


def solution(mesh):
    placed = (
        P("seq", "tp"),
        P("seq", "tp"),
        P("seq", "tp"),
        P("tp", None),
        P(("seq", "tp"), None),
        P("seq", None),
        P("seq"),
        P("seq"),
    )
    return jax.shard_map(
        on_device,
        mesh=mesh,
        in_specs=placed,
        out_specs=(P(("seq", "tp"), None), P("seq", "tp"), P("seq", "tp"), P("seq", "tp")),
        check_vma=False,
    )
```
